32 devices in a mesh: rows: 8 (over y, x, core), cols: 4 (over z).
Axes of the slice: x: 2, y: 2, z: 4, core: 2. Of those that a mesh axis runs over, the one named last changes fastest.
Arguments:
- basis: float32 [512, 4096], P(None, ('cols', 'rows')), may hold values from -6 to 6
- tile_counts: int32 [1024, 128, 128], P(('rows', 'cols')), may hold values from 0 to 63
- tile_rows: int32 [1024], P(('rows', 'cols')), may hold values from 0 to 3
- tile_cols: int32 [1024], P(('rows', 'cols')), may hold values from 0 to 7
- tile_live: int32 [32], P(('rows', 'cols')), may hold values from 8 to 32, as said below
- marginals: int32 [4096], replicated, may hold values from 1 to 983040, as said below
Outputs:
- subspace: float32 [512, 4096], P(None, ('cols', 'rows'))
The draws below stay inside these ranges and needn't reach their ends.
Inputs may be any that keep to these rules, and one draw needn't show every extreme that they name: `tile_live`: every list has at least a quarter of its 32 slots live; some list has all 32 live. `marginals`: A small multiplier times a power of four.
All inputs are finite; a program needn't handle non-finite values.
Results may differ from the reference program's by a relative error of at most 0.012.
The reference program's roundings to bfloat16 on the way (of `ppmi` and `rounded`) count: a program that leaves them out, or rounds other values in their place, can miss the bound.
Values may be sent and summed in bfloat16 or wider, within the bound.
A program may use at most 128 MiB of HBM per device.

```python
import jax
import jax.numpy as jnp
from jax import lax

K = 512
BT = 128
TB_DEV = 128
TILES_DEV = 32
ITERS = 2
VOCAB = 4096
ROWBLK = 4
COLBLK = 8
N_ROWS = 8
N_COLS = 4


def draw_tile_live(key, part):
    key = jax.random.fold_in(key, 11)
    first_key, second_key = jax.random.split(key)
    counted = jax.random.randint(first_key, (N_ROWS * N_COLS,), TILES_DEV // 4, TILES_DEV + 1, dtype=jnp.int32)
    fullest = jax.random.randint(second_key, (), 0, N_ROWS * N_COLS, dtype=jnp.int32)
    return counted.at[fullest].set(TILES_DEV)


def draw_marginals(key, part):
    key = jax.random.fold_in(key, 23)
    first_key, second_key = jax.random.split(key)
    leading = jax.random.randint(first_key, (VOCAB,), 1, 16, dtype=jnp.int32)
    exponents = jax.random.randint(second_key, (VOCAB,), 0, 9, dtype=jnp.int32)
    return leading * jnp.left_shift(jnp.ones_like(exponents), 2 * exponents)


def with_ends(array, own_key, low, top_value):
    place = [jax.random.randint(jax.random.fold_in(own_key, axis), (), 0, length) for axis, length in enumerate(array.shape)]
    main_axis = array.shape.index(max(array.shape))
    neighbour = place[:main_axis] + [(place[main_axis] + 1) % array.shape[main_axis]] + place[main_axis + 1:]
    return array.at[tuple(place)].set(low).at[tuple(neighbour)].set(top_value)


def block_levels(stream_key, extent, shards, low, top_value):
    factor_of = 1.0
    for dim, blocks in shards:
        heights = jax.random.uniform(jax.random.fold_in(jax.random.fold_in(stream_key, 6), dim), (blocks,), jnp.float32, low / len(shards), top_value / len(shards))
        factor_of = factor_of * jnp.repeat(jnp.exp(heights), extent[dim] // blocks).reshape((-1,) + (1,) * (len(extent) - 1 - dim))
    return factor_of


def scatter_about(key, extent, width, limit, pieces=(), kind=jnp.bfloat16):
    result = width * jax.random.normal(key, extent, jnp.float32)
    if pieces:
        result = result * block_levels(key, extent, pieces, -0.22, 0.18)
    return jnp.clip(result, -limit, limit).astype(kind)


def setup_inputs(seed: int = 0) -> dict:
    key_list = jax.random.split(jax.random.key(seed), 7)
    basis = scatter_about(key_list[0], (K, VOCAB), 1.0, 6.0, ((1, 32),), jnp.float32)
    tile_counts = with_ends(jax.random.randint(key_list[1], (N_ROWS * N_COLS * TILES_DEV, BT, BT), 0, 64), jax.random.fold_in(key_list[1], 1), 0, 63).astype(jnp.int32)
    tile_rows = with_ends(jax.random.randint(key_list[2], (N_ROWS * N_COLS * TILES_DEV,), 0, ROWBLK), jax.random.fold_in(key_list[2], 1), 0, ROWBLK - 1).astype(jnp.int32)
    tile_cols = with_ends(jax.random.randint(key_list[3], (N_ROWS * N_COLS * TILES_DEV,), 0, COLBLK), jax.random.fold_in(key_list[3], 1), 0, COLBLK - 1).astype(jnp.int32)
    tile_live = draw_tile_live(jax.random.fold_in(key_list[6], 71), 0)
    marginals = draw_marginals(jax.random.fold_in(key_list[6], 71), 0)
    return dict(basis=basis, tile_counts=tile_counts, tile_rows=tile_rows, tile_cols=tile_cols, tile_live=tile_live, marginals=marginals)


def reference(basis, tile_counts, tile_rows, tile_cols, tile_live, marginals):
    devices_all = N_ROWS * N_COLS
    group_size = N_ROWS * TB_DEV
    row_blocks = N_COLS * TB_DEV // BT
    marg_float = marginals.astype(jnp.float32)
    grand_total = jnp.sum(marg_float)
    log_margins = jnp.log(marg_float)
    stacked_logs = log_margins.reshape(N_COLS, N_ROWS, TB_DEV)
    counts_all = tile_counts.reshape(devices_all, TILES_DEV, BT, BT)
    rows_all = tile_rows.reshape(devices_all, TILES_DEV)
    cols_all = tile_cols.reshape(devices_all, TILES_DEV)
    position = jnp.arange(TILES_DEV, dtype=jnp.int32)
    block_ids = jnp.arange(row_blocks, dtype=jnp.int32)
    current = basis
    for sweep_index in range(ITERS):
        rounded = lax.optimization_barrier(current.astype(jnp.bfloat16))

        def one_device(running, device):
            row_index = device // N_COLS
            col_index = device % N_COLS
            row_logs = lax.dynamic_index_in_dim(stacked_logs, row_index, 1, keepdims=False).reshape(-1, BT)
            col_logs = lax.dynamic_slice_in_dim(log_margins, col_index * group_size, group_size).reshape(-1, BT)
            counts_here = lax.dynamic_index_in_dim(counts_all, device, 0, keepdims=False)
            rows_here = lax.dynamic_index_in_dim(rows_all, device, 0, keepdims=False)
            cols_here = lax.dynamic_index_in_dim(cols_all, device, 0, keepdims=False)
            live_here = lax.dynamic_index_in_dim(tile_live, device, 0, keepdims=False)
            counts_float = counts_here.astype(jnp.float32)
            log_ratio = jnp.log(jnp.maximum(counts_float, 1.0)) + jnp.log(grand_total) - jnp.take(row_logs, rows_here, axis=0)[:, :, None] - jnp.take(col_logs, cols_here, axis=0)[:, None, :]
            keep_mask = (counts_here > 0) & (position < live_here)[:, None, None]
            ppmi = lax.optimization_barrier(jnp.where(keep_mask, jnp.maximum(log_ratio, 0.0), 0.0).astype(jnp.bfloat16))
            group_basis = lax.dynamic_slice_in_dim(rounded, col_index * group_size, group_size, 1).reshape(K, -1, BT)
            picked = jnp.take(group_basis, cols_here, axis=1)
            products = jnp.einsum('ktc,trc->ktr', picked.astype(jnp.float32), ppmi.astype(jnp.float32))
            onehot = (rows_here[:, None] == block_ids[None, :]).astype(jnp.float32)
            placed = jnp.einsum('ktr,ta->kar', products, onehot, precision=lax.Precision.HIGHEST)
            placed = placed.reshape(K, N_COLS, TB_DEV)
            previous = lax.dynamic_index_in_dim(running, row_index, 2, keepdims=False)
            running = lax.dynamic_update_index_in_dim(running, previous + placed, row_index, 2)
            return (running, None)
        zero_sum = jnp.zeros((K, N_COLS, N_ROWS, TB_DEV), jnp.float32)
        summed, unused = lax.scan(one_device, zero_sum, jnp.arange(devices_all, dtype=jnp.int32))
        full_image = summed.reshape(K, N_COLS * N_ROWS * TB_DEV)
        gram_matrix = jnp.dot(full_image.astype(jnp.float32), full_image.T.astype(jnp.float32), precision=lax.Precision.HIGHEST, preferred_element_type=jnp.float32)
        factor = jnp.linalg.cholesky(gram_matrix)
        current = jax.scipy.linalg.solve_triangular(factor, full_image, lower=True)
    return current
```

```python
import functools

import jax
import jax.numpy as jnp
from jax import lax
from jax.experimental import pallas as pl
from jax.experimental.pallas import tpu as pltpu
from jax.sharding import PartitionSpec as P

ITERS = 2
HIGHEST = lax.Precision.HIGHEST
MESH = pl.DeviceIdType.MESH
VMEM = pl.BlockSpec(memory_space=pltpu.VMEM)
SMEM = pl.BlockSpec(memory_space=pltpu.SMEM)
BLOCK = 128
PANEL = 16


def dot_nt(left, right, precision=HIGHEST):
    return lax.dot_general(
        left, right, (((1,), (1,)), ((), ())), precision=precision, preferred_element_type=jnp.float32
    )


def dot_tn(left, right):
    return lax.dot_general(
        left, right, (((0,), (0,)), ((), ())), precision=HIGHEST, preferred_element_type=jnp.float32
    )


def dot_nn(left, right):
    return jnp.dot(left, right, precision=HIGHEST, preferred_element_type=jnp.float32)


def matrix_kernel(rows_ref, cols_ref, live_ref, total_ref, counts_ref, row_logs_ref, col_logs_ref, high_ref, low_ref, dense):
    tile = counts_ref.shape[1]
    log_total = total_ref[0]
    dense[...] = jnp.zeros_like(dense)

    def add_tile(slot, carry):
        row = pl.multiple_of(rows_ref[slot] * tile, tile)
        col = pl.multiple_of(cols_ref[slot] * tile, tile)
        counts = counts_ref[slot]
        ratio = (
            jnp.log(jnp.maximum(counts.astype(jnp.float32), 1.0))
            + log_total
            - row_logs_ref[pl.ds(row, tile), :]
            - col_logs_ref[:, pl.ds(col, tile)]
        )
        value = jnp.where(counts > 0, jnp.maximum(ratio, 0.0), 0.0)
        value = value.astype(jnp.bfloat16).astype(jnp.float32)
        dense[pl.ds(row, tile), pl.ds(col, tile)] += value
        return carry

    lax.fori_loop(0, live_ref[0], add_tile, 0)

    def split(block, carry):
        here = pl.ds(pl.multiple_of(block * tile, tile), tile)
        whole = dense[here, :]
        high = whole.astype(jnp.bfloat16)
        high_ref[here, :] = high
        low_ref[here, :] = (whole - high.astype(jnp.float32)).astype(jnp.bfloat16)
        return carry

    lax.fori_loop(0, dense.shape[0] // tile, split, 0)


def build_matrix(tile_rows, tile_cols, tile_live, log_total, tile_counts, row_logs, col_logs):
    shape = (row_logs.shape[0], col_logs.shape[1])
    return pl.pallas_call(
        matrix_kernel,
        out_shape=[jax.ShapeDtypeStruct(shape, jnp.bfloat16)] * 2,
        in_specs=[SMEM] * 4 + [VMEM] * 3,
        out_specs=[VMEM] * 2,
        scratch_shapes=[pltpu.VMEM(shape, jnp.float32)],
        compiler_params=pltpu.CompilerParams(vmem_limit_bytes=56 * 2**20),
    )(tile_rows, tile_cols, tile_live, log_total, tile_counts, row_logs, col_logs)


def block_pairs(width):
    count = width // BLOCK
    return [(i, j) for i in range(count) for j in range(i, count)]


def gram_kernel(chips, depth, x_ref, sum_ref, mine, core_in, plane_in, z_in, core_send, core_recv, plane_send, plane_recv, z_send, z_recv):
    row = lax.axis_index("rows")
    level = lax.axis_index("cols")
    chip = row // 2
    core = row % 2
    sibling = {"rows": chip * 2 + (1 - core), "cols": level}
    plane = [{"rows": lax.rem(chip + k, chips) * 2 + core, "cols": level} for k in range(1, chips)]
    column = [{"rows": row, "cols": lax.rem(level + k, depth)} for k in range(1, depth)]
    peers = [sibling] + plane + column
    barrier = pltpu.get_barrier_semaphore()
    for peer in peers:
        pl.semaphore_signal(barrier, inc=1, device_id=peer, device_id_type=MESH)

    total = mine.shape[0]
    half = total // 2
    piece = half // chips
    part = piece // depth
    pairs = block_pairs(x_ref.shape[0])
    for index, (i, j) in enumerate(pairs):
        mine[index * BLOCK : (index + 1) * BLOCK, :] = dot_nt(
            x_ref[i * BLOCK : (i + 1) * BLOCK, :], x_ref[j * BLOCK : (j + 1) * BLOCK, :]
        )
    used = len(pairs) * BLOCK
    if used < total:
        mine[used:, :] = jnp.zeros((total - used, BLOCK), jnp.float32)
    pl.semaphore_wait(barrier, len(peers))

    def rows_at(start, size):
        return pl.ds(pl.multiple_of(start, 8), size)

    def send(source, target, sends, receives, index, peer):
        copy = pltpu.make_async_remote_copy(
            src_ref=source,
            dst_ref=target,
            send_sem=sends.at[index],
            recv_sem=receives.at[index],
            device_id=peer,
            device_id_type=MESH,
        )
        copy.start()
        return copy

    half_start = core * half
    copy = send(mine.at[rows_at((1 - core) * half, half)], core_in, core_send, core_recv, 0, sibling)
    copy.wait()
    mine[rows_at(half_start, half), :] += core_in[...]

    piece_start = half_start + chip * piece
    copies = [
        send(mine.at[rows_at(half_start + lax.rem(chip + k, chips) * piece, piece)], plane_in.at[k - 1], plane_send, plane_recv, k - 1, plane[k - 1])
        for k in range(1, chips)
    ]
    for copy in copies:
        copy.wait()
    summed = mine[rows_at(piece_start, piece), :]
    for k in range(1, chips):
        summed += plane_in[k - 1]
    mine[rows_at(piece_start, piece), :] = summed

    part_start = piece_start + level * part
    copies = [
        send(mine.at[rows_at(piece_start + lax.rem(level + k, depth) * part, part)], z_in.at[k - 1], z_send, z_recv, k - 1, column[k - 1])
        for k in range(1, depth)
    ]
    for copy in copies:
        copy.wait()
    summed = mine[rows_at(part_start, part), :]
    for k in range(1, depth):
        summed += z_in[k - 1]
    sum_ref[rows_at(part_start, part), :] = summed

    here = sum_ref.at[rows_at(part_start, part)]
    copies = [
        send(here, here, z_send, z_recv, depth - 2 + k, column[k - 1]) for k in range(1, depth)
    ]
    for copy in copies:
        copy.wait()
    here = sum_ref.at[rows_at(piece_start, piece)]
    copies = [
        send(here, here, plane_send, plane_recv, chips - 2 + k, plane[k - 1]) for k in range(1, chips)
    ]
    for copy in copies:
        copy.wait()
    here = sum_ref.at[rows_at(half_start, half)]
    send(here, here, core_send, core_recv, 1, sibling).wait()


def gram_sum(share):
    chips = lax.axis_size("rows") // 2
    depth = lax.axis_size("cols")
    unit = 8 * 2 * chips * depth
    used = len(block_pairs(share.shape[0])) * BLOCK
    total = -(-used // unit) * unit
    half = total // 2
    piece = half // chips
    part = piece // depth
    dma = pltpu.SemaphoreType.DMA
    return pl.pallas_call(
        functools.partial(gram_kernel, chips, depth),
        out_shape=jax.ShapeDtypeStruct((total, BLOCK), jnp.float32),
        in_specs=[VMEM],
        out_specs=VMEM,
        scratch_shapes=[
            pltpu.VMEM((total, BLOCK), jnp.float32),
            pltpu.VMEM((half, BLOCK), jnp.float32),
            pltpu.VMEM((chips - 1, piece, BLOCK), jnp.float32),
            pltpu.VMEM((depth - 1, part, BLOCK), jnp.float32),
            dma((2,)),
            dma((2,)),
            dma((2 * (chips - 1),)),
            dma((2 * (chips - 1),)),
            dma((2 * (depth - 1),)),
            dma((2 * (depth - 1),)),
        ],
        compiler_params=pltpu.CompilerParams(
            collective_id=0, has_side_effects=True, vmem_limit_bytes=32 * 2**20
        ),
    )(share)


def solve_kernel(gram_ref, x_ref, y_ref, work, small):
    width = x_ref.shape[0]
    count = width // BLOCK
    for index, (i, j) in enumerate(block_pairs(width)):
        work[i * BLOCK : (i + 1) * BLOCK, j * BLOCK : (j + 1) * BLOCK] = gram_ref[index * BLOCK : (index + 1) * BLOCK, :]
    work[:, width:] = x_ref[...]
    below = lax.broadcasted_iota(jnp.int32, (PANEL, BLOCK), 0)
    unit = (
        lax.broadcasted_iota(jnp.int32, (BLOCK, BLOCK), 0) == lax.broadcasted_iota(jnp.int32, (BLOCK, BLOCK), 1)
    ).astype(jnp.float32)

    def one_block(b, carry):
        here = pl.ds(pl.multiple_of(b * BLOCK, BLOCK), BLOCK)
        small[:, :BLOCK] = work[here, here]
        small[:, BLOCK:] = unit
        for start in range(0, BLOCK, PANEL):
            left = small[start : start + PANEL, :BLOCK]
            right = small[start : start + PANEL, BLOCK:]
            lanes = [
                jnp.broadcast_to(left[:, start + k : start + k + 1], (PANEL, BLOCK)) for k in range(PANEL)
            ]
            for i in range(PANEL):
                inverse = lax.rsqrt(lanes[i][i : i + 1, :])
                left_row = left[i : i + 1, :] * inverse
                right_row = right[i : i + 1, :] * inverse
                scale = jnp.where(below > i, lanes[i] * inverse, 0.0)
                left = jnp.where(below == i, left_row, left - scale * left_row)
                right = jnp.where(below == i, right_row, right - scale * right_row)
                for k in range(i + 1, PANEL):
                    lanes[k] = lanes[k] - scale * (lanes[k][i : i + 1, :] * inverse)
            small[start : start + PANEL, :BLOCK] = left
            small[start : start + PANEL, BLOCK:] = right
            rest = start + PANEL
            if rest < BLOCK:
                both = small[start : start + PANEL, :]
                small[rest:, :] -= dot_tn(left, both)[rest:, :]
        solved = dot_nn(small[:, BLOCK:], work[here, :])
        work[here, :] = solved
        y_ref[here, :] = solved[:, width:]

        def update(i, inner):
            there = pl.ds(pl.multiple_of(i * BLOCK, BLOCK), BLOCK)
            work[there, :] -= dot_tn(work[here, there], work[here, :])
            return inner

        lax.fori_loop(b + 1, count, update, 0)
        return carry

    lax.fori_loop(0, count, one_block, 0)


def solve(gram, share):
    width, terms = share.shape
    return pl.pallas_call(
        solve_kernel,
        out_shape=jax.ShapeDtypeStruct(share.shape, jnp.float32),
        in_specs=[VMEM] * 2,
        out_specs=VMEM,
        scratch_shapes=[
            pltpu.VMEM((width, width + terms), jnp.float32),
            pltpu.VMEM((BLOCK, 2 * BLOCK), jnp.float32),
        ],
        compiler_params=pltpu.CompilerParams(vmem_limit_bytes=32 * 2**20),
    )(gram, share)


def local(basis, tile_counts, tile_rows, tile_cols, tile_live, marginals):
    terms_here = basis.shape[1]
    row_count = lax.axis_size("rows")
    col_count = lax.axis_size("cols")
    row_index = lax.axis_index("rows")
    col_index = lax.axis_index("cols")
    group_size = row_count * terms_here
    marg_float = marginals.astype(jnp.float32)
    log_total = jnp.log(jnp.sum(marg_float)).reshape(1)
    log_margins = jnp.log(marg_float)
    row_logs = lax.dynamic_index_in_dim(
        log_margins.reshape(col_count, row_count, terms_here), row_index, 1, keepdims=False
    ).reshape(-1, 1)
    col_logs = lax.dynamic_slice_in_dim(log_margins, col_index * group_size, group_size).reshape(1, -1)
    high, low = build_matrix(tile_rows, tile_cols, tile_live, log_total, tile_counts, row_logs, col_logs)
    current = basis
    for _ in range(ITERS):
        gathered = lax.all_gather(current.astype(jnp.bfloat16), "rows", axis=1, tiled=True)
        partial_sum = dot_nt(gathered, high, None) + dot_nt(gathered, low, None)
        share = lax.psum_scatter(partial_sum, "cols", scatter_dimension=1, tiled=True)
        current = solve(gram_sum(share), share)
    return current


def solution(mesh):
    in_specs = (
        P(None, ("cols", "rows")),
        P(("rows", "cols"), None, None),
        P(("rows", "cols")),
        P(("rows", "cols")),
        P(("rows", "cols")),
        P(),
    )
    out_specs = P(None, ("cols", "rows"))
    return jax.shard_map(local, mesh=mesh, in_specs=in_specs, out_specs=out_specs, check_vma=False)
```

```python
import functools

import jax
import jax.numpy as jnp
from jax import lax
from jax.experimental import pallas as pl
from jax.experimental.pallas import tpu as pltpu
from jax.sharding import PartitionSpec as P

ITERS = 2
HIGHEST = lax.Precision.HIGHEST
MESH = pl.DeviceIdType.MESH
VMEM = pl.BlockSpec(memory_space=pltpu.VMEM)
SMEM = pl.BlockSpec(memory_space=pltpu.SMEM)
BLOCK = 128
PANEL = 16
CHUNKS = 4


def dot_nt(left, right, precision=HIGHEST):
    return lax.dot_general(
        left, right, (((1,), (1,)), ((), ())), precision=precision, preferred_element_type=jnp.float32
    )


def dot_tn(left, right):
    return lax.dot_general(
        left, right, (((0,), (0,)), ((), ())), precision=HIGHEST, preferred_element_type=jnp.float32
    )


def dot_nn(left, right):
    return jnp.dot(left, right, precision=HIGHEST, preferred_element_type=jnp.float32)


def matrix_kernel(rows_ref, cols_ref, live_ref, total_ref, counts_ref, row_logs_ref, col_logs_ref, high_ref, low_ref, dense):
    tile = counts_ref.shape[1]
    log_total = total_ref[0]
    dense[...] = jnp.zeros_like(dense)

    def add_tile(slot, carry):
        row = pl.multiple_of(rows_ref[slot] * tile, tile)
        col = pl.multiple_of(cols_ref[slot] * tile, tile)
        counts = counts_ref[slot]
        ratio = (
            jnp.log(jnp.maximum(counts.astype(jnp.float32), 1.0))
            + log_total
            - row_logs_ref[pl.ds(row, tile), :]
            - col_logs_ref[:, pl.ds(col, tile)]
        )
        value = jnp.where(counts > 0, jnp.maximum(ratio, 0.0), 0.0)
        value = value.astype(jnp.bfloat16).astype(jnp.float32)
        dense[pl.ds(row, tile), pl.ds(col, tile)] += value
        return carry

    lax.fori_loop(0, live_ref[0], add_tile, 0)

    def split(block, carry):
        here = pl.ds(pl.multiple_of(block * tile, tile), tile)
        whole = dense[here, :]
        high = whole.astype(jnp.bfloat16)
        high_ref[here, :] = high
        low_ref[here, :] = (whole - high.astype(jnp.float32)).astype(jnp.bfloat16)
        return carry

    lax.fori_loop(0, dense.shape[0] // tile, split, 0)


def build_matrix(tile_rows, tile_cols, tile_live, log_total, tile_counts, row_logs, col_logs):
    shape = (row_logs.shape[0], col_logs.shape[1])
    return pl.pallas_call(
        matrix_kernel,
        out_shape=[jax.ShapeDtypeStruct(shape, jnp.bfloat16)] * 2,
        in_specs=[SMEM] * 4 + [VMEM] * 3,
        out_specs=[VMEM] * 2,
        scratch_shapes=[pltpu.VMEM(shape, jnp.float32)],
        compiler_params=pltpu.CompilerParams(vmem_limit_bytes=56 * 2**20),
    )(tile_rows, tile_cols, tile_live, log_total, tile_counts, row_logs, col_logs)


def block_pairs(width):
    count = width // BLOCK
    return [(i, j) for i in range(count) for j in range(i, count)]


def sweep_kernel(
    chips, depth, cur_ref, high_ref, low_ref, share_ref, sum_ref,
    basis, part, up_in, down_in, mine, core_in, plane_in, z_in,
    near_send, near_recv, far_send, far_recv, pass_send, pass_recv, up_send, up_recv, down_send, down_recv,
    core_send, core_recv, plane_send, plane_recv, z_send, z_recv,
):
    row = lax.axis_index("rows")
    level = lax.axis_index("cols")
    chip = row // 2
    core = row % 2
    sibling = {"rows": chip * 2 + (1 - core), "cols": level}
    plane = [{"rows": lax.rem(chip + k, chips) * 2 + core, "cols": level} for k in range(1, chips)]
    column = [{"rows": row, "cols": lax.rem(level + k, depth)} for k in range(1, depth)]
    peers = [sibling] + plane + column
    above, below = column[0], column[depth - 2]
    barrier = pltpu.get_barrier_semaphore()
    for peer in peers:
        pl.semaphore_signal(barrier, inc=1, device_id=peer, device_id_type=MESH)
    width, terms = cur_ref.shape
    lanes = pl.ds(pl.multiple_of(core * terms, terms), terms)
    basis[chip, :, lanes] = cur_ref[...].astype(jnp.bfloat16)
    pl.semaphore_wait(barrier, len(peers))

    def rows_at(start, size):
        return pl.ds(pl.multiple_of(start, 8), size)

    def remote(source, target, sends, receives, index, peer):
        return pltpu.make_async_remote_copy(
            src_ref=source,
            dst_ref=target,
            send_sem=sends.at[index],
            recv_sem=receives.at[index],
            device_id=peer,
            device_id_type=MESH,
        )

    def send(*description):
        copy = remote(*description)
        copy.start()
        return copy

    chunk = width // CHUNKS
    others = chips - 1
    near, far = [], []
    for q in range(CHUNKS):
        own = basis.at[chip, q * chunk : (q + 1) * chunk, lanes]
        far.append([send(own, own, far_send, far_recv, q * others + k, plane[k]) for k in range(others)])
        near.append(send(own, own, near_send, near_recv, q, sibling))

    def up_copy(q, l):
        return remote(part.at[q, l], up_in.at[q, l], up_send, up_recv, q * depth + l, above)

    def down_copy(q, l):
        return remote(part.at[q, l], down_in.at[q, l], down_send, down_recv, q * depth + l, below)

    pair = 2 * terms
    passed_on = []
    for q in range(CHUNKS):
        passed = []
        for k in range(others):
            far[q][k].wait_recv()
            there = basis.at[lax.rem(chip + chips - k - 1, chips), q * chunk : (q + 1) * chunk, lanes]
            passed.append(send(there, there, pass_send, pass_recv, q * others + k, sibling))
        passed_on += passed
        near[q].wait_recv()
        total = None
        for k in range(chips):
            if k:
                passed[k - 1].wait_recv()
            source = lax.rem(chip + chips - k, chips)
            columns = pl.ds(pl.multiple_of(source * pair, pair), pair)
            vectors = basis[source, q * chunk : (q + 1) * chunk, :]
            product = dot_nt(vectors, high_ref[:, columns], None) + dot_nt(vectors, low_ref[:, columns], None)
            total = product if total is None else total + product
        for l in range(depth):
            part[q, l] = total[:, l * terms : (l + 1) * terms]

        @pl.when(level == 0)
        def _():
            for l in range(depth - 1, 0, -1):
                up_copy(q, l).start()

        @pl.when(level == depth - 1)
        def _():
            for l in range(depth - 1):
                down_copy(q, l).start()

    for q in range(CHUNKS):
        for s in range(depth - 1):
            l = depth - 1 - s

            @pl.when((level > 0) & (level <= l))
            def _():
                up_copy(q, l).wait_recv()
                part[q, l] += up_in[q, l]

            @pl.when((level > 0) & (level < l))
            def _():
                up_copy(q, l).start()

            @pl.when((level < depth - 1) & (level >= s))
            def _():
                down_copy(q, s).wait_recv()
                part[q, s] += down_in[q, s]

            @pl.when((level < depth - 1) & (level > s))
            def _():
                down_copy(q, s).start()

        share_ref[q * chunk : (q + 1) * chunk, :] = part[q, level]

    total = mine.shape[0]
    half = total // 2
    piece = half // chips
    portion = piece // depth
    pairs = block_pairs(width)
    for index, (i, j) in enumerate(pairs):
        mine[index * BLOCK : (index + 1) * BLOCK, :] = dot_nt(
            share_ref[i * BLOCK : (i + 1) * BLOCK, :], share_ref[j * BLOCK : (j + 1) * BLOCK, :]
        )
    used = len(pairs) * BLOCK
    if used < total:
        mine[used:, :] = jnp.zeros((total - used, BLOCK), jnp.float32)

    half_start = core * half
    first = send(mine.at[rows_at((1 - core) * half, half)], core_in, core_send, core_recv, 0, sibling)
    for q in range(CHUNKS):
        near[q].wait_send()
        for k in range(others):
            far[q][k].wait_send()
        for l in range(depth):

            @pl.when(level < l)
            def _():
                up_copy(q, l).wait_send()

            @pl.when(level > l)
            def _():
                down_copy(q, l).wait_send()

    for copy in passed_on:
        copy.wait_send()
    first.wait()
    mine[rows_at(half_start, half), :] += core_in[...]

    piece_start = half_start + chip * piece
    copies = [
        send(mine.at[rows_at(half_start + lax.rem(chip + k, chips) * piece, piece)], plane_in.at[k - 1], plane_send, plane_recv, k - 1, plane[k - 1])
        for k in range(1, chips)
    ]
    for copy in copies:
        copy.wait()
    summed = mine[rows_at(piece_start, piece), :]
    for k in range(1, chips):
        summed += plane_in[k - 1]
    mine[rows_at(piece_start, piece), :] = summed

    part_start = piece_start + level * portion
    copies = [
        send(mine.at[rows_at(piece_start + lax.rem(level + k, depth) * portion, portion)], z_in.at[k - 1], z_send, z_recv, k - 1, column[k - 1])
        for k in range(1, depth)
    ]
    for copy in copies:
        copy.wait()
    summed = mine[rows_at(part_start, portion), :]
    for k in range(1, depth):
        summed += z_in[k - 1]
    sum_ref[rows_at(part_start, portion), :] = summed

    here = sum_ref.at[rows_at(part_start, portion)]
    copies = [
        send(here, here, z_send, z_recv, depth - 2 + k, column[k - 1]) for k in range(1, depth)
    ]
    for copy in copies:
        copy.wait()
    here = sum_ref.at[rows_at(piece_start, piece)]
    copies = [
        send(here, here, plane_send, plane_recv, chips - 2 + k, plane[k - 1]) for k in range(1, chips)
    ]
    for copy in copies:
        copy.wait()
    here = sum_ref.at[rows_at(half_start, half)]
    send(here, here, core_send, core_recv, 1, sibling).wait()


def sweep(current, high, low):
    chips = lax.axis_size("rows") // 2
    depth = lax.axis_size("cols")
    width, terms = current.shape
    chunk = width // CHUNKS
    unit = 8 * 2 * chips * depth
    used = len(block_pairs(width)) * BLOCK
    total = -(-used // unit) * unit
    half = total // 2
    piece = half // chips
    portion = piece // depth
    floats = lambda *shape: pltpu.VMEM(shape, jnp.float32)
    counts = [CHUNKS, CHUNKS * (chips - 1), CHUNKS * (chips - 1), CHUNKS * depth, CHUNKS * depth, 2, 2 * (chips - 1), 2 * (depth - 1)]
    return pl.pallas_call(
        functools.partial(sweep_kernel, chips, depth),
        out_shape=[
            jax.ShapeDtypeStruct((width, terms), jnp.float32),
            jax.ShapeDtypeStruct((total, BLOCK), jnp.float32),
        ],
        in_specs=[VMEM] * 3,
        out_specs=[VMEM] * 2,
        scratch_shapes=[
            pltpu.VMEM((chips, width, 2 * terms), jnp.bfloat16),
            floats(CHUNKS, depth, chunk, terms),
            floats(CHUNKS, depth, chunk, terms),
            floats(CHUNKS, depth, chunk, terms),
            floats(total, BLOCK),
            floats(half, BLOCK),
            floats(chips - 1, piece, BLOCK),
            floats(depth - 1, portion, BLOCK),
        ]
        + [pltpu.SemaphoreType.DMA((count,)) for count in counts for _ in range(2)],
        compiler_params=pltpu.CompilerParams(
            collective_id=0, has_side_effects=True, vmem_limit_bytes=56 * 2**20
        ),
    )(current, high, low)


def solve_kernel(gram_ref, x_ref, y_ref, work, small):
    width = x_ref.shape[0]
    count = width // BLOCK
    for index, (i, j) in enumerate(block_pairs(width)):
        work[i * BLOCK : (i + 1) * BLOCK, j * BLOCK : (j + 1) * BLOCK] = gram_ref[index * BLOCK : (index + 1) * BLOCK, :]
    work[:, width:] = x_ref[...]
    below = lax.broadcasted_iota(jnp.int32, (PANEL, BLOCK), 0)
    unit = (
        lax.broadcasted_iota(jnp.int32, (BLOCK, BLOCK), 0) == lax.broadcasted_iota(jnp.int32, (BLOCK, BLOCK), 1)
    ).astype(jnp.float32)

    def one_block(b, carry):
        here = pl.ds(pl.multiple_of(b * BLOCK, BLOCK), BLOCK)
        small[:, :BLOCK] = work[here, here]
        small[:, BLOCK:] = unit
        for start in range(0, BLOCK, PANEL):
            left = small[start : start + PANEL, :BLOCK]
            right = small[start : start + PANEL, BLOCK:]
            lanes = [
                jnp.broadcast_to(left[:, start + k : start + k + 1], (PANEL, BLOCK)) for k in range(PANEL)
            ]
            for i in range(PANEL):
                inverse = lax.rsqrt(lanes[i][i : i + 1, :])
                left_row = left[i : i + 1, :] * inverse
                right_row = right[i : i + 1, :] * inverse
                scale = jnp.where(below > i, lanes[i] * inverse, 0.0)
                left = jnp.where(below == i, left_row, left - scale * left_row)
                right = jnp.where(below == i, right_row, right - scale * right_row)
                for k in range(i + 1, PANEL):
                    lanes[k] = lanes[k] - scale * (lanes[k][i : i + 1, :] * inverse)
            small[start : start + PANEL, :BLOCK] = left
            small[start : start + PANEL, BLOCK:] = right
            rest = start + PANEL
            if rest < BLOCK:
                both = small[start : start + PANEL, :]
                small[rest:, :] -= dot_tn(left, both)[rest:, :]
        solved = dot_nn(small[:, BLOCK:], work[here, :])
        work[here, :] = solved
        y_ref[here, :] = solved[:, width:]

        def update(i, inner):
            there = pl.ds(pl.multiple_of(i * BLOCK, BLOCK), BLOCK)
            work[there, :] -= dot_tn(work[here, there], work[here, :])
            return inner

        lax.fori_loop(b + 1, count, update, 0)
        return carry

    lax.fori_loop(0, count, one_block, 0)


def solve(gram, share):
    width, terms = share.shape
    return pl.pallas_call(
        solve_kernel,
        out_shape=jax.ShapeDtypeStruct(share.shape, jnp.float32),
        in_specs=[VMEM] * 2,
        out_specs=VMEM,
        scratch_shapes=[
            pltpu.VMEM((width, width + terms), jnp.float32),
            pltpu.VMEM((BLOCK, 2 * BLOCK), jnp.float32),
        ],
        compiler_params=pltpu.CompilerParams(vmem_limit_bytes=32 * 2**20),
    )(gram, share)


def local(basis, tile_counts, tile_rows, tile_cols, tile_live, marginals):
    terms_here = basis.shape[1]
    row_count = lax.axis_size("rows")
    col_count = lax.axis_size("cols")
    row_index = lax.axis_index("rows")
    col_index = lax.axis_index("cols")
    group_size = row_count * terms_here
    marg_float = marginals.astype(jnp.float32)
    log_total = jnp.log(jnp.sum(marg_float)).reshape(1)
    log_margins = jnp.log(marg_float)
    row_logs = lax.dynamic_index_in_dim(
        log_margins.reshape(col_count, row_count, terms_here), row_index, 1, keepdims=False
    ).reshape(-1, 1)
    col_logs = lax.dynamic_slice_in_dim(log_margins, col_index * group_size, group_size).reshape(1, -1)
    high, low = build_matrix(tile_rows, tile_cols, tile_live, log_total, tile_counts, row_logs, col_logs)
    current = basis
    for _ in range(ITERS):
        share, gram = sweep(current, high, low)
        current = solve(gram, share)
    return current


def solution(mesh):
    in_specs = (
        P(None, ("cols", "rows")),
        P(("rows", "cols"), None, None),
        P(("rows", "cols")),
        P(("rows", "cols")),
        P(("rows", "cols")),
        P(),
    )
    out_specs = P(None, ("cols", "rows"))
    return jax.shard_map(local, mesh=mesh, in_specs=in_specs, out_specs=out_specs, check_vma=False)
```

```python
import functools

import jax
import jax.numpy as jnp
from jax import lax
from jax.experimental import pallas as pl
from jax.experimental.pallas import tpu as pltpu
from jax.sharding import PartitionSpec as P

ITERS = 2
HIGHEST = lax.Precision.HIGHEST
MESH = pl.DeviceIdType.MESH
VMEM = pl.BlockSpec(memory_space=pltpu.VMEM)
SMEM = pl.BlockSpec(memory_space=pltpu.SMEM)
BLOCK = 128
PANEL = 16
CHUNKS = 4


def dot_nt(left, right, precision=HIGHEST):
    return lax.dot_general(
        left, right, (((1,), (1,)), ((), ())), precision=precision, preferred_element_type=jnp.float32
    )


def dot_tn(left, right):
    return lax.dot_general(
        left, right, (((0,), (0,)), ((), ())), precision=HIGHEST, preferred_element_type=jnp.float32
    )


def dot_nn(left, right):
    return jnp.dot(left, right, precision=HIGHEST, preferred_element_type=jnp.float32)


def matrix_kernel(rows_ref, cols_ref, live_ref, total_ref, counts_ref, row_logs_ref, col_logs_ref, high_ref, low_ref, dense):
    tile = counts_ref.shape[1]
    log_total = total_ref[0]
    dense[...] = jnp.zeros_like(dense)

    def add_tile(slot, carry):
        row = pl.multiple_of(rows_ref[slot] * tile, tile)
        col = pl.multiple_of(cols_ref[slot] * tile, tile)
        counts = counts_ref[slot]
        ratio = (
            jnp.log(jnp.maximum(counts.astype(jnp.float32), 1.0))
            + log_total
            - row_logs_ref[pl.ds(row, tile), :]
            - col_logs_ref[:, pl.ds(col, tile)]
        )
        value = jnp.where(counts > 0, jnp.maximum(ratio, 0.0), 0.0)
        value = value.astype(jnp.bfloat16).astype(jnp.float32)
        dense[pl.ds(row, tile), pl.ds(col, tile)] += value
        return carry

    lax.fori_loop(0, live_ref[0], add_tile, 0)

    def split(block, carry):
        here = pl.ds(pl.multiple_of(block * tile, tile), tile)
        whole = dense[here, :]
        high = whole.astype(jnp.bfloat16)
        high_ref[here, :] = high
        low_ref[here, :] = (whole - high.astype(jnp.float32)).astype(jnp.bfloat16)
        return carry

    lax.fori_loop(0, dense.shape[0] // tile, split, 0)


def build_matrix(tile_rows, tile_cols, tile_live, log_total, tile_counts, row_logs, col_logs):
    shape = (row_logs.shape[0], col_logs.shape[1])
    return pl.pallas_call(
        matrix_kernel,
        out_shape=[jax.ShapeDtypeStruct(shape, jnp.bfloat16)] * 2,
        in_specs=[SMEM] * 4 + [VMEM] * 3,
        out_specs=[VMEM] * 2,
        scratch_shapes=[pltpu.VMEM(shape, jnp.float32)],
        compiler_params=pltpu.CompilerParams(vmem_limit_bytes=56 * 2**20),
    )(tile_rows, tile_cols, tile_live, log_total, tile_counts, row_logs, col_logs)


def block_pairs(width):
    count = width // BLOCK
    return [(i, j) for i in range(count) for j in range(i, count)]


def sweep_kernel(
    chips, depth, cur_ref, high_ref, low_ref, share_ref, sum_ref,
    basis, part, inbox, relay, mine, core_in, plane_in, z_in,
    near_send, near_recv, far_send, far_recv, pass_send, pass_recv, sum_send, sum_recv, relay_send, relay_recv,
    core_send, core_recv, plane_send, plane_recv, z_send, z_recv,
):
    row = lax.axis_index("rows")
    level = lax.axis_index("cols")
    chip = row // 2
    core = row % 2
    sibling = {"rows": chip * 2 + (1 - core), "cols": level}
    plane = [{"rows": lax.rem(chip + k, chips) * 2 + core, "cols": level} for k in range(1, chips)]
    column = [{"rows": row, "cols": lax.rem(level + k, depth)} for k in range(1, depth)]
    peers = [sibling] + plane + column
    above, below = column[0], column[depth - 2]
    barrier = pltpu.get_barrier_semaphore()
    for peer in peers:
        pl.semaphore_signal(barrier, inc=1, device_id=peer, device_id_type=MESH)
    width, terms = cur_ref.shape
    lanes = pl.ds(pl.multiple_of(core * terms, terms), terms)
    basis[chip, :, lanes] = cur_ref[...].astype(jnp.bfloat16)
    pl.semaphore_wait(barrier, len(peers))

    def rows_at(start, size):
        return pl.ds(pl.multiple_of(start, 8), size)

    def remote(source, target, sent, received, peer):
        return pltpu.make_async_remote_copy(
            src_ref=source,
            dst_ref=target,
            send_sem=sent,
            recv_sem=received,
            device_id=peer,
            device_id_type=MESH,
        )

    def send(source, target, sends, receives, index, peer):
        copy = remote(source, target, sends.at[index], receives.at[index], peer)
        copy.start()
        return copy

    chunk = width // CHUNKS
    others = chips - 1
    near, far = [], []
    for q in range(CHUNKS):
        own = basis.at[chip, q * chunk : (q + 1) * chunk, lanes]
        far.append([send(own, own, far_send, far_recv, q * others + k, plane[k]) for k in range(others)])
        near.append(send(own, own, near_send, near_recv, q, sibling))

    last = depth - 1

    def direct_copy(q, k):
        return remote(part.at[q, lax.rem(level + k, depth)], inbox.at[q, level], sum_send.at[q * depth + k], sum_recv.at[q * depth + level], column[k - 1])

    def relay_copy(q, target, peer):
        return remote(part.at[q, target], relay.at[q], relay_send.at[q], relay_recv.at[q], peer)

    def waits_for_relay(k):
        target = lax.rem(level + k, depth)
        return ((level <= 1) & (target == last)) | ((level >= last - 1) & (target == 0))

    pair = 2 * terms
    passed_on = []
    for q in range(CHUNKS):
        passed = []
        for k in range(others):
            far[q][k].wait_recv()
            there = basis.at[lax.rem(chip + chips - k - 1, chips), q * chunk : (q + 1) * chunk, lanes]
            passed.append(send(there, there, pass_send, pass_recv, q * others + k, sibling))
        passed_on += passed
        near[q].wait_recv()
        total = None
        for k in range(chips):
            if k:
                passed[k - 1].wait_recv()
            source = lax.rem(chip + chips - k, chips)
            columns = pl.ds(pl.multiple_of(source * pair, pair), pair)
            vectors = basis[source, q * chunk : (q + 1) * chunk, :]
            product = dot_nt(vectors, high_ref[:, columns], None) + dot_nt(vectors, low_ref[:, columns], None)
            total = product if total is None else total + product
        for l in range(depth):
            part[q, l] = total[:, l * terms : (l + 1) * terms]

        @pl.when(level == 0)
        def _():
            relay_copy(q, last, above).start()

        @pl.when(level == last)
        def _():
            relay_copy(q, 0, below).start()

        for k in range(1, depth):

            @pl.when(jnp.logical_not(waits_for_relay(k)))
            def _():
                direct_copy(q, k).start()

    for q in range(CHUNKS):

        @pl.when(level == 1)
        def _():
            relay_copy(q, last, above).wait_recv()
            part[q, last] += relay[q]
            direct_copy(q, last - 1).start()

        @pl.when(level == last - 1)
        def _():
            relay_copy(q, 0, below).wait_recv()
            part[q, 0] += relay[q]
            direct_copy(q, 2).start()

    for q in range(CHUNKS):
        here = slice(q * chunk, (q + 1) * chunk)
        share_ref[here, :] = part[q, level]
        for u in range(depth):
            absent = (level == u) | ((level == last) & (u == 0)) | ((level == 0) & (u == last))

            @pl.when(jnp.logical_not(absent))
            def _():
                remote(part.at[q, u], inbox.at[q, u], sum_send.at[q * depth], sum_recv.at[q * depth + u], above).wait_recv()
                share_ref[here, :] += inbox[q, u]

    total = mine.shape[0]
    half = total // 2
    piece = half // chips
    portion = piece // depth
    pairs = block_pairs(width)
    for index, (i, j) in enumerate(pairs):
        mine[index * BLOCK : (index + 1) * BLOCK, :] = dot_nt(
            share_ref[i * BLOCK : (i + 1) * BLOCK, :], share_ref[j * BLOCK : (j + 1) * BLOCK, :]
        )
    used = len(pairs) * BLOCK
    if used < total:
        mine[used:, :] = jnp.zeros((total - used, BLOCK), jnp.float32)

    half_start = core * half
    first = send(mine.at[rows_at((1 - core) * half, half)], core_in, core_send, core_recv, 0, sibling)
    for q in range(CHUNKS):
        near[q].wait_send()
        for k in range(others):
            far[q][k].wait_send()
        for k in range(1, depth):
            by_relay = ((level == 0) & (k == last)) | ((level == last) & (k == 1))

            @pl.when(jnp.logical_not(by_relay))
            def _():
                direct_copy(q, k).wait_send()

        @pl.when(level == 0)
        def _():
            relay_copy(q, last, above).wait_send()

        @pl.when(level == last)
        def _():
            relay_copy(q, 0, below).wait_send()

    for copy in passed_on:
        copy.wait_send()
    first.wait()
    mine[rows_at(half_start, half), :] += core_in[...]

    piece_start = half_start + chip * piece
    copies = [
        send(mine.at[rows_at(half_start + lax.rem(chip + k, chips) * piece, piece)], plane_in.at[k - 1], plane_send, plane_recv, k - 1, plane[k - 1])
        for k in range(1, chips)
    ]
    for copy in copies:
        copy.wait()
    summed = mine[rows_at(piece_start, piece), :]
    for k in range(1, chips):
        summed += plane_in[k - 1]
    mine[rows_at(piece_start, piece), :] = summed

    part_start = piece_start + level * portion
    copies = [
        send(mine.at[rows_at(piece_start + lax.rem(level + k, depth) * portion, portion)], z_in.at[k - 1], z_send, z_recv, k - 1, column[k - 1])
        for k in range(1, depth)
    ]
    for copy in copies:
        copy.wait()
    summed = mine[rows_at(part_start, portion), :]
    for k in range(1, depth):
        summed += z_in[k - 1]
    sum_ref[rows_at(part_start, portion), :] = summed

    here = sum_ref.at[rows_at(part_start, portion)]
    copies = [
        send(here, here, z_send, z_recv, depth - 2 + k, column[k - 1]) for k in range(1, depth)
    ]
    for copy in copies:
        copy.wait()
    here = sum_ref.at[rows_at(piece_start, piece)]
    copies = [
        send(here, here, plane_send, plane_recv, chips - 2 + k, plane[k - 1]) for k in range(1, chips)
    ]
    for copy in copies:
        copy.wait()
    here = sum_ref.at[rows_at(half_start, half)]
    send(here, here, core_send, core_recv, 1, sibling).wait()


def sweep(current, high, low):
    chips = lax.axis_size("rows") // 2
    depth = lax.axis_size("cols")
    width, terms = current.shape
    chunk = width // CHUNKS
    unit = 8 * 2 * chips * depth
    used = len(block_pairs(width)) * BLOCK
    total = -(-used // unit) * unit
    half = total // 2
    piece = half // chips
    portion = piece // depth
    floats = lambda *shape: pltpu.VMEM(shape, jnp.float32)
    counts = [CHUNKS, CHUNKS * (chips - 1), CHUNKS * (chips - 1), CHUNKS * depth, CHUNKS, 2, 2 * (chips - 1), 2 * (depth - 1)]
    return pl.pallas_call(
        functools.partial(sweep_kernel, chips, depth),
        out_shape=[
            jax.ShapeDtypeStruct((width, terms), jnp.float32),
            jax.ShapeDtypeStruct((total, BLOCK), jnp.float32),
        ],
        in_specs=[VMEM] * 3,
        out_specs=[VMEM] * 2,
        scratch_shapes=[
            pltpu.VMEM((chips, width, 2 * terms), jnp.bfloat16),
            floats(CHUNKS, depth, chunk, terms),
            floats(CHUNKS, depth, chunk, terms),
            floats(CHUNKS, chunk, terms),
            floats(total, BLOCK),
            floats(half, BLOCK),
            floats(chips - 1, piece, BLOCK),
            floats(depth - 1, portion, BLOCK),
        ]
        + [pltpu.SemaphoreType.DMA((count,)) for count in counts for _ in range(2)],
        compiler_params=pltpu.CompilerParams(
            collective_id=0, has_side_effects=True, vmem_limit_bytes=56 * 2**20
        ),
    )(current, high, low)


def solve_kernel(gram_ref, x_ref, y_ref, work, small):
    width = x_ref.shape[0]
    count = width // BLOCK
    for index, (i, j) in enumerate(block_pairs(width)):
        work[i * BLOCK : (i + 1) * BLOCK, j * BLOCK : (j + 1) * BLOCK] = gram_ref[index * BLOCK : (index + 1) * BLOCK, :]
    work[:, width:] = x_ref[...]
    below = lax.broadcasted_iota(jnp.int32, (PANEL, BLOCK), 0)
    unit = (
        lax.broadcasted_iota(jnp.int32, (BLOCK, BLOCK), 0) == lax.broadcasted_iota(jnp.int32, (BLOCK, BLOCK), 1)
    ).astype(jnp.float32)

    def one_block(b, carry):
        here = pl.ds(pl.multiple_of(b * BLOCK, BLOCK), BLOCK)
        small[:, :BLOCK] = work[here, here]
        small[:, BLOCK:] = unit
        for start in range(0, BLOCK, PANEL):
            left = small[start : start + PANEL, :BLOCK]
            right = small[start : start + PANEL, BLOCK:]
            lanes = [
                jnp.broadcast_to(left[:, start + k : start + k + 1], (PANEL, BLOCK)) for k in range(PANEL)
            ]
            for i in range(PANEL):
                inverse = lax.rsqrt(lanes[i][i : i + 1, :])
                left_row = left[i : i + 1, :] * inverse
                right_row = right[i : i + 1, :] * inverse
                scale = jnp.where(below > i, lanes[i] * inverse, 0.0)
                left = jnp.where(below == i, left_row, left - scale * left_row)
                right = jnp.where(below == i, right_row, right - scale * right_row)
                for k in range(i + 1, PANEL):
                    lanes[k] = lanes[k] - scale * (lanes[k][i : i + 1, :] * inverse)
            small[start : start + PANEL, :BLOCK] = left
            small[start : start + PANEL, BLOCK:] = right
            rest = start + PANEL
            if rest < BLOCK:
                both = small[start : start + PANEL, :]
                small[rest:, :] -= dot_tn(left, both)[rest:, :]
        solved = dot_nn(small[:, BLOCK:], work[here, :])
        work[here, :] = solved
        y_ref[here, :] = solved[:, width:]

        def update(i, inner):
            there = pl.ds(pl.multiple_of(i * BLOCK, BLOCK), BLOCK)
            work[there, :] -= dot_tn(work[here, there], work[here, :])
            return inner

        lax.fori_loop(b + 1, count, update, 0)
        return carry

    lax.fori_loop(0, count, one_block, 0)


def solve(gram, share):
    width, terms = share.shape
    return pl.pallas_call(
        solve_kernel,
        out_shape=jax.ShapeDtypeStruct(share.shape, jnp.float32),
        in_specs=[VMEM] * 2,
        out_specs=VMEM,
        scratch_shapes=[
            pltpu.VMEM((width, width + terms), jnp.float32),
            pltpu.VMEM((BLOCK, 2 * BLOCK), jnp.float32),
        ],
        compiler_params=pltpu.CompilerParams(vmem_limit_bytes=32 * 2**20),
    )(gram, share)


def local(basis, tile_counts, tile_rows, tile_cols, tile_live, marginals):
    terms_here = basis.shape[1]
    row_count = lax.axis_size("rows")
    col_count = lax.axis_size("cols")
    row_index = lax.axis_index("rows")
    col_index = lax.axis_index("cols")
    group_size = row_count * terms_here
    marg_float = marginals.astype(jnp.float32)
    log_total = jnp.log(jnp.sum(marg_float)).reshape(1)
    log_margins = jnp.log(marg_float)
    row_logs = lax.dynamic_index_in_dim(
        log_margins.reshape(col_count, row_count, terms_here), row_index, 1, keepdims=False
    ).reshape(-1, 1)
    col_logs = lax.dynamic_slice_in_dim(log_margins, col_index * group_size, group_size).reshape(1, -1)
    high, low = build_matrix(tile_rows, tile_cols, tile_live, log_total, tile_counts, row_logs, col_logs)
    current = basis
    for _ in range(ITERS):
        share, gram = sweep(current, high, low)
        current = solve(gram, share)
    return current


def solution(mesh):
    in_specs = (
        P(None, ("cols", "rows")),
        P(("rows", "cols"), None, None),
        P(("rows", "cols")),
        P(("rows", "cols")),
        P(("rows", "cols")),
        P(),
    )
    out_specs = P(None, ("cols", "rows"))
    return jax.shard_map(local, mesh=mesh, in_specs=in_specs, out_specs=out_specs, check_vma=False)
```

```python
import functools

import jax
import jax.numpy as jnp
from jax import lax
from jax.experimental import pallas as pl
from jax.experimental.pallas import tpu as pltpu
from jax.sharding import PartitionSpec as P

ITERS = 2
HIGHEST = lax.Precision.HIGHEST
MESH = pl.DeviceIdType.MESH
VMEM = pl.BlockSpec(memory_space=pltpu.VMEM)
SMEM = pl.BlockSpec(memory_space=pltpu.SMEM)
BLOCK = 128
PANEL = 16


def dot_nt(left, right, precision=HIGHEST):
    return lax.dot_general(
        left, right, (((1,), (1,)), ((), ())), precision=precision, preferred_element_type=jnp.float32
    )


def dot_tn(left, right):
    return lax.dot_general(
        left, right, (((0,), (0,)), ((), ())), precision=HIGHEST, preferred_element_type=jnp.float32
    )


def dot_nn(left, right):
    return jnp.dot(left, right, precision=HIGHEST, preferred_element_type=jnp.float32)


def matrix_kernel(rows_ref, cols_ref, live_ref, total_ref, counts_ref, row_logs_ref, col_logs_ref, high_ref, low_ref, dense):
    tile = counts_ref.shape[1]
    log_total = total_ref[0]
    dense[...] = jnp.zeros_like(dense)

    def add_tile(slot, carry):
        row = pl.multiple_of(rows_ref[slot] * tile, tile)
        col = pl.multiple_of(cols_ref[slot] * tile, tile)
        counts = counts_ref[slot]
        ratio = (
            jnp.log(jnp.maximum(counts.astype(jnp.float32), 1.0))
            + log_total
            - row_logs_ref[pl.ds(row, tile), :]
            - col_logs_ref[:, pl.ds(col, tile)]
        )
        value = jnp.where(counts > 0, jnp.maximum(ratio, 0.0), 0.0)
        value = value.astype(jnp.bfloat16).astype(jnp.float32)
        dense[pl.ds(row, tile), pl.ds(col, tile)] += value
        return carry

    lax.fori_loop(0, live_ref[0], add_tile, 0)

    def split(block, carry):
        here = pl.ds(pl.multiple_of(block * tile, tile), tile)
        whole = dense[here, :]
        high = whole.astype(jnp.bfloat16)
        high_ref[here, :] = high
        low_ref[here, :] = (whole - high.astype(jnp.float32)).astype(jnp.bfloat16)
        return carry

    lax.fori_loop(0, dense.shape[0] // tile, split, 0)


def build_matrix(tile_rows, tile_cols, tile_live, log_total, tile_counts, row_logs, col_logs):
    shape = (row_logs.shape[0], col_logs.shape[1])
    return pl.pallas_call(
        matrix_kernel,
        out_shape=[jax.ShapeDtypeStruct(shape, jnp.bfloat16)] * 2,
        in_specs=[SMEM] * 4 + [VMEM] * 3,
        out_specs=[VMEM] * 2,
        scratch_shapes=[pltpu.VMEM(shape, jnp.float32)],
        compiler_params=pltpu.CompilerParams(vmem_limit_bytes=56 * 2**20),
    )(tile_rows, tile_cols, tile_live, log_total, tile_counts, row_logs, col_logs)


def block_pairs(width):
    count = width // BLOCK
    return [(i, j) for i in range(count) for j in range(i, count)]


def iterate_kernel(chips, depth, cur_ref, high_ref, low_ref, out_ref, share, work, small, *rounds):
    row = lax.axis_index("rows")
    level = lax.axis_index("cols")
    chip = row // 2
    core = row % 2
    sibling = {"rows": chip * 2 + (1 - core), "cols": level}
    plane = [{"rows": lax.rem(chip + k, chips) * 2 + core, "cols": level} for k in range(1, chips)]
    column = [{"rows": row, "cols": lax.rem(level + k, depth)} for k in range(1, depth)]
    peers = [sibling] + plane + column
    above, below = column[0], column[depth - 2]
    barrier = pltpu.get_barrier_semaphore()
    for peer in peers:
        pl.semaphore_signal(barrier, inc=1, device_id=peer, device_id_type=MESH)
    width, terms = cur_ref.shape
    chunk = BLOCK
    chunks = width // chunk
    others = chips - 1
    last = depth - 1
    pair = 2 * terms
    pairs = block_pairs(width)
    lanes = pl.ds(pl.multiple_of(core * terms, terms), terms)

    def rows_at(start, size):
        return pl.ds(pl.multiple_of(start, 8), size)

    def block_at(index):
        return pl.ds(pl.multiple_of(index * BLOCK, BLOCK), BLOCK)

    def remote(source, target, sent, received, peer):
        return pltpu.make_async_remote_copy(
            src_ref=source,
            dst_ref=target,
            send_sem=sent,
            recv_sem=received,
            device_id=peer,
            device_id_type=MESH,
        )

    def send(source, target, sends, receives, index, peer):
        copy = remote(source, target, sends.at[index], receives.at[index], peer)
        copy.start()
        return copy

    def each(count, step):
        def body(index, carry):
            step(index)
            return carry

        lax.fori_loop(0, count, body, 0)

    def make_round(
        basis, part, inbox, relay, mine, core_in, plane_in, z_in, gram,
        near_send, near_recv, far_send, far_recv, pass_send, pass_recv, sum_send, sum_recv, relay_send, relay_recv,
        core_send, core_recv, plane_send, plane_recv, z_send, z_recv,
    ):
        def near_copy(q):
            own = basis.at[chip, block_at(q), lanes]
            return remote(own, own, near_send.at[q], near_recv.at[q], sibling)

        def far_copy(q, k):
            own = basis.at[chip, block_at(q), lanes]
            index = q * others + k
            return remote(own, own, far_send.at[index], far_recv.at[index], plane[k])

        def pass_copy(q, k):
            there = basis.at[lax.rem(chip + others - k, chips), block_at(q), lanes]
            index = q * others + k
            return remote(there, there, pass_send.at[index], pass_recv.at[index], sibling)

        def direct_copy(q, k):
            return remote(part.at[q, lax.rem(level + k, depth)], inbox.at[q, level], sum_send.at[q * depth + k], sum_recv.at[q * depth + level], column[k - 1])

        def relay_copy(q, target, peer):
            return remote(part.at[q, target], relay.at[q], relay_send.at[q], relay_recv.at[q], peer)

        def gather(q, vectors):
            basis[chip, block_at(q), lanes] = vectors.astype(jnp.bfloat16)
            for k in range(others):
                far_copy(q, k).start()
            near_copy(q).start()

        def multiply(q):
            for k in range(others):
                far_copy(q, k).wait_recv()
                pass_copy(q, k).start()
            near_copy(q).wait_recv()
            total = None
            for k in range(chips):
                if k:
                    pass_copy(q, k - 1).wait_recv()
                source = lax.rem(chip + chips - k, chips)
                columns = pl.ds(pl.multiple_of(source * pair, pair), pair)
                vectors = basis[source, block_at(q), :]
                product = dot_nt(vectors, high_ref[:, columns], None) + dot_nt(vectors, low_ref[:, columns], None)
                total = product if total is None else total + product
            for l in range(depth):
                part[q, l] = total[:, l * terms : (l + 1) * terms]

            @pl.when(level == 0)
            def _():
                relay_copy(q, last, above).start()

            @pl.when(level == last)
            def _():
                relay_copy(q, 0, below).start()

            for k in range(1, depth):
                target = lax.rem(level + k, depth)
                waits = ((level <= 1) & (target == last)) | ((level >= last - 1) & (target == 0))

                @pl.when(jnp.logical_not(waits))
                def _():
                    direct_copy(q, k).start()

        def pass_relay(q):
            @pl.when(level == 1)
            def _():
                relay_copy(q, last, above).wait_recv()
                part[q, last] += relay[q]
                direct_copy(q, last - 1).start()

            @pl.when(level == last - 1)
            def _():
                relay_copy(q, 0, below).wait_recv()
                part[q, 0] += relay[q]
                direct_copy(q, 2).start()

        def collect(q):
            share[block_at(q), :] = part[q, level]
            for u in range(depth):
                absent = (level == u) | ((level == last) & (u == 0)) | ((level == 0) & (u == last))

                @pl.when(jnp.logical_not(absent))
                def _():
                    remote(part.at[q, u], inbox.at[q, u], sum_send.at[q * depth], sum_recv.at[q * depth + u], above).wait_recv()
                    share[block_at(q), :] += inbox[q, u]

        def wait_sent(q):
            near_copy(q).wait_send()
            for k in range(others):
                far_copy(q, k).wait_send()
                pass_copy(q, k).wait_send()
            for k in range(1, depth):
                by_relay = ((level == 0) & (k == last)) | ((level == last) & (k == 1))

                @pl.when(jnp.logical_not(by_relay))
                def _():
                    direct_copy(q, k).wait_send()

            @pl.when(level == 0)
            def _():
                relay_copy(q, last, above).wait_send()

            @pl.when(level == last)
            def _():
                relay_copy(q, 0, below).wait_send()

        def reduce_gram():
            total = mine.shape[0]
            half = total // 2
            piece = half // chips
            portion = piece // depth
            for index, (i, j) in enumerate(pairs):
                mine[index * BLOCK : (index + 1) * BLOCK, :] = dot_nt(
                    share[i * BLOCK : (i + 1) * BLOCK, :], share[j * BLOCK : (j + 1) * BLOCK, :]
                )
            used = len(pairs) * BLOCK
            if used < total:
                mine[used:, :] = jnp.zeros((total - used, BLOCK), jnp.float32)

            half_start = core * half
            first = send(mine.at[rows_at((1 - core) * half, half)], core_in, core_send, core_recv, 0, sibling)
            each(chunks, wait_sent)
            first.wait()
            mine[rows_at(half_start, half), :] += core_in[...]

            piece_start = half_start + chip * piece
            copies = [
                send(mine.at[rows_at(half_start + lax.rem(chip + k, chips) * piece, piece)], plane_in.at[k - 1], plane_send, plane_recv, k - 1, plane[k - 1])
                for k in range(1, chips)
            ]
            for copy in copies:
                copy.wait()
            summed = mine[rows_at(piece_start, piece), :]
            for k in range(1, chips):
                summed += plane_in[k - 1]
            mine[rows_at(piece_start, piece), :] = summed

            part_start = piece_start + level * portion
            copies = [
                send(mine.at[rows_at(piece_start + lax.rem(level + k, depth) * portion, portion)], z_in.at[k - 1], z_send, z_recv, k - 1, column[k - 1])
                for k in range(1, depth)
            ]
            for copy in copies:
                copy.wait()
            summed = mine[rows_at(part_start, portion), :]
            for k in range(1, depth):
                summed += z_in[k - 1]
            gram[rows_at(part_start, portion), :] = summed

            here = gram.at[rows_at(part_start, portion)]
            copies = [
                send(here, here, z_send, z_recv, depth - 2 + k, column[k - 1]) for k in range(1, depth)
            ]
            for copy in copies:
                copy.wait()
            here = gram.at[rows_at(piece_start, piece)]
            copies = [
                send(here, here, plane_send, plane_recv, chips - 2 + k, plane[k - 1]) for k in range(1, chips)
            ]
            for copy in copies:
                copy.wait()
            here = gram.at[rows_at(half_start, half)]
            send(here, here, core_send, core_recv, 1, sibling).wait()
            for index, (i, j) in enumerate(pairs):
                work[i * BLOCK : (i + 1) * BLOCK, j * BLOCK : (j + 1) * BLOCK] = gram[index * BLOCK : (index + 1) * BLOCK, :]
            work[:, width:] = share[...]

        return gather, multiply, pass_relay, collect, reduce_gram

    sublane = lax.broadcasted_iota(jnp.int32, (PANEL, BLOCK), 0)
    unit = (
        lax.broadcasted_iota(jnp.int32, (BLOCK, BLOCK), 0) == lax.broadcasted_iota(jnp.int32, (BLOCK, BLOCK), 1)
    ).astype(jnp.float32)

    def eliminate(b):
        here = block_at(b)
        small[:, :BLOCK] = work[here, here]
        small[:, BLOCK:] = unit
        for start in range(0, BLOCK, PANEL):
            left = small[start : start + PANEL, :BLOCK]
            right = small[start : start + PANEL, BLOCK:]
            spread = [
                jnp.broadcast_to(left[:, start + k : start + k + 1], (PANEL, BLOCK)) for k in range(PANEL)
            ]
            for i in range(PANEL):
                inverse = lax.rsqrt(spread[i][i : i + 1, :])
                left_row = left[i : i + 1, :] * inverse
                right_row = right[i : i + 1, :] * inverse
                scale = jnp.where(sublane > i, spread[i] * inverse, 0.0)
                left = jnp.where(sublane == i, left_row, left - scale * left_row)
                right = jnp.where(sublane == i, right_row, right - scale * right_row)
                for k in range(i + 1, PANEL):
                    spread[k] = spread[k] - scale * (spread[k][i : i + 1, :] * inverse)
            small[start : start + PANEL, :BLOCK] = left
            small[start : start + PANEL, BLOCK:] = right
            rest = start + PANEL
            if rest < BLOCK:
                both = small[start : start + PANEL, :]
                small[rest:, :] -= dot_tn(left, both)[rest:, :]
        solved = dot_nn(small[:, BLOCK:], work[here, :])
        work[here, :] = solved
        return solved[:, width:]

    def update(b):
        def body(i, carry):
            work[block_at(i), :] -= dot_tn(work[block_at(b), block_at(i)], work[block_at(b), :])
            return carry

        lax.fori_loop(b + 1, chunks, body, 0)

    per = len(rounds) // ITERS
    parts = [make_round(*rounds[it * per : (it + 1) * per]) for it in range(ITERS)]
    pl.semaphore_wait(barrier, len(peers))
    gather, multiply = parts[0][:2]
    each(chunks, lambda q: gather(q, cur_ref[block_at(q), :]))
    each(chunks, multiply)
    for it in range(ITERS):
        pass_relay, collect, reduce_gram = parts[it][2:]
        each(chunks, pass_relay)
        each(chunks, collect)
        reduce_gram()
        if it + 1 < ITERS:
            gather, multiply = parts[it + 1][:2]

            def step(b):
                gather(b, eliminate(b))
                update(b)

                @pl.when(b > 0)
                def _():
                    multiply(b - 1)

            each(chunks, step)
            multiply(chunks - 1)
        else:

            def final(b):
                out_ref[block_at(b), :] = eliminate(b)
                update(b)

            each(chunks, final)


def iterate(current, high, low):
    chips = lax.axis_size("rows") // 2
    depth = lax.axis_size("cols")
    width, terms = current.shape
    chunks = width // BLOCK
    unit = 8 * 2 * chips * depth
    used = len(block_pairs(width)) * BLOCK
    total = -(-used // unit) * unit
    half = total // 2
    piece = half // chips
    portion = piece // depth

    def floats(*shape):
        return pltpu.VMEM(shape, jnp.float32)

    counts = [chunks, chunks * (chips - 1), chunks * (chips - 1), chunks * depth, chunks, 2, 2 * (chips - 1), 2 * (depth - 1)]
    one_round = [
        pltpu.VMEM((chips, width, 2 * terms), jnp.bfloat16),
        floats(chunks, depth, BLOCK, terms),
        floats(chunks, depth, BLOCK, terms),
        floats(chunks, BLOCK, terms),
        floats(total, BLOCK),
        floats(half, BLOCK),
        floats(chips - 1, piece, BLOCK),
        floats(depth - 1, portion, BLOCK),
        floats(total, BLOCK),
    ] + [pltpu.SemaphoreType.DMA((count,)) for count in counts for _ in range(2)]
    return pl.pallas_call(
        functools.partial(iterate_kernel, chips, depth),
        out_shape=jax.ShapeDtypeStruct((width, terms), jnp.float32),
        in_specs=[VMEM] * 3,
        out_specs=VMEM,
        scratch_shapes=[floats(width, terms), floats(width, width + terms), floats(BLOCK, 2 * BLOCK)] + one_round * ITERS,
        compiler_params=pltpu.CompilerParams(
            collective_id=0, has_side_effects=True, vmem_limit_bytes=56 * 2**20
        ),
    )(current, high, low)


def local(basis, tile_counts, tile_rows, tile_cols, tile_live, marginals):
    terms_here = basis.shape[1]
    row_count = lax.axis_size("rows")
    col_count = lax.axis_size("cols")
    row_index = lax.axis_index("rows")
    col_index = lax.axis_index("cols")
    group_size = row_count * terms_here
    marg_float = marginals.astype(jnp.float32)
    log_total = jnp.log(jnp.sum(marg_float)).reshape(1)
    log_margins = jnp.log(marg_float)
    row_logs = lax.dynamic_index_in_dim(
        log_margins.reshape(col_count, row_count, terms_here), row_index, 1, keepdims=False
    ).reshape(-1, 1)
    col_logs = lax.dynamic_slice_in_dim(log_margins, col_index * group_size, group_size).reshape(1, -1)
    high, low = build_matrix(tile_rows, tile_cols, tile_live, log_total, tile_counts, row_logs, col_logs)
    return iterate(basis, high, low)


def solution(mesh):
    in_specs = (
        P(None, ("cols", "rows")),
        P(("rows", "cols"), None, None),
        P(("rows", "cols")),
        P(("rows", "cols")),
        P(("rows", "cols")),
        P(),
    )
    out_specs = P(None, ("cols", "rows"))
    return jax.shard_map(local, mesh=mesh, in_specs=in_specs, out_specs=out_specs, check_vma=False)
```

```python
import functools

import jax
import jax.numpy as jnp
from jax import lax
from jax.experimental import pallas as pl
from jax.experimental.pallas import tpu as pltpu
from jax.sharding import PartitionSpec as P

ITERS = 2
HIGHEST = lax.Precision.HIGHEST
MESH = pl.DeviceIdType.MESH
VMEM = pl.BlockSpec(memory_space=pltpu.VMEM)
SMEM = pl.BlockSpec(memory_space=pltpu.SMEM)
BLOCK = 128
PANEL = 16


def dot_nt(left, right, precision=HIGHEST):
    return lax.dot_general(
        left, right, (((1,), (1,)), ((), ())), precision=precision, preferred_element_type=jnp.float32
    )


def dot_tn(left, right):
    return lax.dot_general(
        left, right, (((0,), (0,)), ((), ())), precision=HIGHEST, preferred_element_type=jnp.float32
    )


def dot_nn(left, right):
    return jnp.dot(left, right, precision=HIGHEST, preferred_element_type=jnp.float32)


def matrix_kernel(rows_ref, cols_ref, live_ref, total_ref, counts_ref, row_logs_ref, col_logs_ref, high_ref, low_ref, dense):
    tile = counts_ref.shape[1]
    log_total = total_ref[0]
    dense[...] = jnp.zeros_like(dense)

    def add_tile(slot, carry):
        row = pl.multiple_of(rows_ref[slot] * tile, tile)
        col = pl.multiple_of(cols_ref[slot] * tile, tile)
        counts = counts_ref[slot]
        ratio = (
            jnp.log(jnp.maximum(counts.astype(jnp.float32), 1.0))
            + log_total
            - row_logs_ref[pl.ds(row, tile), :]
            - col_logs_ref[:, pl.ds(col, tile)]
        )
        value = jnp.where(counts > 0, jnp.maximum(ratio, 0.0), 0.0)
        value = value.astype(jnp.bfloat16).astype(jnp.float32)
        dense[pl.ds(row, tile), pl.ds(col, tile)] += value
        return carry

    lax.fori_loop(0, live_ref[0], add_tile, 0)

    def split(block, carry):
        here = pl.ds(pl.multiple_of(block * tile, tile), tile)
        whole = dense[here, :]
        high = whole.astype(jnp.bfloat16)
        high_ref[here, :] = high
        low_ref[here, :] = (whole - high.astype(jnp.float32)).astype(jnp.bfloat16)
        return carry

    lax.fori_loop(0, dense.shape[0] // tile, split, 0)


def build_matrix(tile_rows, tile_cols, tile_live, log_total, tile_counts, row_logs, col_logs):
    shape = (row_logs.shape[0], col_logs.shape[1])
    return pl.pallas_call(
        matrix_kernel,
        out_shape=[jax.ShapeDtypeStruct(shape, jnp.bfloat16)] * 2,
        in_specs=[SMEM] * 4 + [VMEM] * 3,
        out_specs=[VMEM] * 2,
        scratch_shapes=[pltpu.VMEM(shape, jnp.float32)],
        compiler_params=pltpu.CompilerParams(vmem_limit_bytes=56 * 2**20),
    )(tile_rows, tile_cols, tile_live, log_total, tile_counts, row_logs, col_logs)


def block_pairs(width):
    count = width // BLOCK
    return [(i, j) for i in range(count) for j in range(i, count)]


def iterate_kernel(chips, depth, cur_ref, high_ref, low_ref, out_ref, share, work, small, *rounds):
    row = lax.axis_index("rows")
    level = lax.axis_index("cols")
    chip = row // 2
    core = row % 2
    sibling = {"rows": chip * 2 + (1 - core), "cols": level}
    plane = [{"rows": lax.rem(chip + k, chips) * 2 + core, "cols": level} for k in range(1, chips)]
    column = [{"rows": row, "cols": lax.rem(level + k, depth)} for k in range(1, depth)]
    peers = [sibling] + plane + column
    above, below = column[0], column[depth - 2]
    barrier = pltpu.get_barrier_semaphore()
    for peer in peers:
        pl.semaphore_signal(barrier, inc=1, device_id=peer, device_id_type=MESH)
    width, terms = cur_ref.shape
    chunk = BLOCK
    chunks = width // chunk
    others = chips - 1
    last = depth - 1
    pair = 2 * terms
    pairs = block_pairs(width)
    lanes = pl.ds(pl.multiple_of(core * terms, terms), terms)

    def rows_at(start, size):
        return pl.ds(pl.multiple_of(start, 8), size)

    def block_at(index):
        return pl.ds(pl.multiple_of(index * BLOCK, BLOCK), BLOCK)

    def remote(source, target, sent, received, peer):
        return pltpu.make_async_remote_copy(
            src_ref=source,
            dst_ref=target,
            send_sem=sent,
            recv_sem=received,
            device_id=peer,
            device_id_type=MESH,
        )

    def send(source, target, sends, receives, index, peer):
        copy = remote(source, target, sends.at[index], receives.at[index], peer)
        copy.start()
        return copy

    def each(count, step):
        def body(index, carry):
            step(index)
            return carry

        lax.fori_loop(0, count, body, 0)

    def make_round(
        basis, part, inbox, relay, mine, core_in, plane_in, z_in, gram,
        near_send, near_recv, far_send, far_recv, pass_send, pass_recv, sum_send, sum_recv, relay_send, relay_recv,
        core_send, core_recv, plane_send, plane_recv, z_send, z_recv,
    ):
        def near_copy(q):
            own = basis.at[chip, block_at(q), lanes]
            return remote(own, own, near_send.at[q], near_recv.at[q], sibling)

        def far_copy(q, k):
            own = basis.at[chip, block_at(q), lanes]
            index = q * others + k
            return remote(own, own, far_send.at[index], far_recv.at[index], plane[k])

        def pass_copy(q, k):
            there = basis.at[lax.rem(chip + others - k, chips), block_at(q), lanes]
            index = q * others + k
            return remote(there, there, pass_send.at[index], pass_recv.at[index], sibling)

        def direct_copy(q, k):
            return remote(part.at[q, lax.rem(level + k, depth)], inbox.at[q, level], sum_send.at[q * depth + k], sum_recv.at[q * depth + level], column[k - 1])

        def relay_copy(q, target, peer):
            return remote(part.at[q, target], relay.at[q], relay_send.at[q], relay_recv.at[q], peer)

        def gather(q, vectors):
            basis[chip, block_at(q), lanes] = vectors.astype(jnp.bfloat16)
            for k in range(others):
                far_copy(q, k).start()
            near_copy(q).start()

        def forward(q):
            for k in range(others):
                far_copy(q, k).wait_recv()
                pass_copy(q, k).start()

        def multiply(q):
            near_copy(q).wait_recv()
            total = None
            for k in range(chips):
                if k:
                    pass_copy(q, k - 1).wait_recv()
                source = lax.rem(chip + chips - k, chips)
                columns = pl.ds(pl.multiple_of(source * pair, pair), pair)
                vectors = basis[source, block_at(q), :]
                product = dot_nt(high_ref[:, columns], vectors, None) + dot_nt(low_ref[:, columns], vectors, None)
                total = product if total is None else total + product
            for l in range(depth):
                part[q, l] = total[l * terms : (l + 1) * terms, :]

            @pl.when(level == 0)
            def _():
                relay_copy(q, last, above).start()

            @pl.when(level == last)
            def _():
                relay_copy(q, 0, below).start()

            for k in range(1, depth):
                target = lax.rem(level + k, depth)
                waits = ((level <= 1) & (target == last)) | ((level >= last - 1) & (target == 0))

                @pl.when(jnp.logical_not(waits))
                def _():
                    direct_copy(q, k).start()

        def pass_relay(q):
            @pl.when(level == 1)
            def _():
                relay_copy(q, last, above).wait_recv()
                part[q, last] += relay[q]
                direct_copy(q, last - 1).start()

            @pl.when(level == last - 1)
            def _():
                relay_copy(q, 0, below).wait_recv()
                part[q, 0] += relay[q]
                direct_copy(q, 2).start()

        def collect(q):
            share[block_at(q), :] = part[q, level]
            for u in range(depth):
                absent = (level == u) | ((level == last) & (u == 0)) | ((level == 0) & (u == last))

                @pl.when(jnp.logical_not(absent))
                def _():
                    remote(part.at[q, u], inbox.at[q, u], sum_send.at[q * depth], sum_recv.at[q * depth + u], above).wait_recv()
                    share[block_at(q), :] += inbox[q, u]

            share[block_at(q), :] = share[block_at(q), :].T

        def wait_sent(q):
            near_copy(q).wait_send()
            for k in range(others):
                far_copy(q, k).wait_send()
                pass_copy(q, k).wait_send()
            for k in range(1, depth):
                by_relay = ((level == 0) & (k == last)) | ((level == last) & (k == 1))

                @pl.when(jnp.logical_not(by_relay))
                def _():
                    direct_copy(q, k).wait_send()

            @pl.when(level == 0)
            def _():
                relay_copy(q, last, above).wait_send()

            @pl.when(level == last)
            def _():
                relay_copy(q, 0, below).wait_send()

        def reduce_gram():
            total = mine.shape[0]
            half = total // 2
            piece = half // chips
            portion = piece // depth
            for index, (i, j) in enumerate(pairs):
                mine[index * BLOCK : (index + 1) * BLOCK, :] = dot_nt(
                    share[i * BLOCK : (i + 1) * BLOCK, :], share[j * BLOCK : (j + 1) * BLOCK, :]
                )
            used = len(pairs) * BLOCK
            if used < total:
                mine[used:, :] = jnp.zeros((total - used, BLOCK), jnp.float32)

            half_start = core * half
            first = send(mine.at[rows_at((1 - core) * half, half)], core_in, core_send, core_recv, 0, sibling)
            each(chunks, wait_sent)
            first.wait()
            mine[rows_at(half_start, half), :] += core_in[...]

            piece_start = half_start + chip * piece
            copies = [
                send(mine.at[rows_at(half_start + lax.rem(chip + k, chips) * piece, piece)], plane_in.at[k - 1], plane_send, plane_recv, k - 1, plane[k - 1])
                for k in range(1, chips)
            ]
            for copy in copies:
                copy.wait()
            summed = mine[rows_at(piece_start, piece), :]
            for k in range(1, chips):
                summed += plane_in[k - 1]
            mine[rows_at(piece_start, piece), :] = summed

            part_start = piece_start + level * portion
            copies = [
                send(mine.at[rows_at(piece_start + lax.rem(level + k, depth) * portion, portion)], z_in.at[k - 1], z_send, z_recv, k - 1, column[k - 1])
                for k in range(1, depth)
            ]
            for copy in copies:
                copy.wait()
            summed = mine[rows_at(part_start, portion), :]
            for k in range(1, depth):
                summed += z_in[k - 1]
            gram[rows_at(part_start, portion), :] = summed

            here = gram.at[rows_at(part_start, portion)]
            copies = [
                send(here, here, z_send, z_recv, depth - 2 + k, column[k - 1]) for k in range(1, depth)
            ]
            for copy in copies:
                copy.wait()
            here = gram.at[rows_at(piece_start, piece)]
            copies = [
                send(here, here, plane_send, plane_recv, chips - 2 + k, plane[k - 1]) for k in range(1, chips)
            ]
            for copy in copies:
                copy.wait()
            here = gram.at[rows_at(half_start, half)]
            send(here, here, core_send, core_recv, 1, sibling).wait()
            for index, (i, j) in enumerate(pairs):
                work[i * BLOCK : (i + 1) * BLOCK, j * BLOCK : (j + 1) * BLOCK] = gram[index * BLOCK : (index + 1) * BLOCK, :]
            work[:, width:] = share[...]

        return gather, forward, multiply, pass_relay, collect, reduce_gram

    sublane = lax.broadcasted_iota(jnp.int32, (PANEL, BLOCK), 0)
    unit = (
        lax.broadcasted_iota(jnp.int32, (BLOCK, BLOCK), 0) == lax.broadcasted_iota(jnp.int32, (BLOCK, BLOCK), 1)
    ).astype(jnp.float32)

    def eliminate(b):
        here = block_at(b)
        small[:, :BLOCK] = work[here, here]
        small[:, BLOCK:] = unit
        for start in range(0, BLOCK, PANEL):
            left = small[start : start + PANEL, :BLOCK]
            right = small[start : start + PANEL, BLOCK:]
            spread = [
                jnp.broadcast_to(left[:, start + k : start + k + 1], (PANEL, BLOCK)) for k in range(PANEL)
            ]
            for i in range(PANEL):
                inverse = lax.rsqrt(spread[i][i : i + 1, :])
                left_row = left[i : i + 1, :] * inverse
                right_row = right[i : i + 1, :] * inverse
                scale = jnp.where(sublane > i, spread[i] * inverse, 0.0)
                left = jnp.where(sublane == i, left_row, left - scale * left_row)
                right = jnp.where(sublane == i, right_row, right - scale * right_row)
                for k in range(i + 1, PANEL):
                    spread[k] = spread[k] - scale * (spread[k][i : i + 1, :] * inverse)
            small[start : start + PANEL, :BLOCK] = left
            small[start : start + PANEL, BLOCK:] = right
            rest = start + PANEL
            if rest < BLOCK:
                both = small[start : start + PANEL, :]
                small[rest:, :] -= dot_tn(left, both)[rest:, :]
        solved = dot_nn(small[:, BLOCK:], work[here, :])
        work[here, :] = solved
        return solved[:, width:]

    def update(b):
        def body(i, carry):
            work[block_at(i), :] -= dot_tn(work[block_at(b), block_at(i)], work[block_at(b), :])
            return carry

        lax.fori_loop(b + 1, chunks, body, 0)

    per = len(rounds) // ITERS
    parts = [make_round(*rounds[it * per : (it + 1) * per]) for it in range(ITERS)]
    pl.semaphore_wait(barrier, len(peers))
    gather, forward, multiply = parts[0][:3]
    each(chunks, lambda q: gather(q, cur_ref[block_at(q), :]))
    forward(0)

    def first_step(q):
        forward(q + 1)
        multiply(q)

    each(chunks - 1, first_step)
    multiply(chunks - 1)
    for it in range(ITERS):
        pass_relay, collect, reduce_gram = parts[it][3:]
        each(chunks, pass_relay)
        each(chunks, collect)
        reduce_gram()
        if it + 1 < ITERS:
            gather, forward, multiply = parts[it + 1][:3]

            def step(b):
                solved = eliminate(b)
                gather(b, solved)

                @pl.when(b > 0)
                def _():
                    forward(b - 1)

                update(b)

                @pl.when(b > 0)
                def _():
                    multiply(b - 1)

            each(chunks, step)
            forward(chunks - 1)
            multiply(chunks - 1)
        else:

            def final(b):
                out_ref[block_at(b), :] = eliminate(b)
                update(b)

            each(chunks, final)


def iterate(current, high, low):
    chips = lax.axis_size("rows") // 2
    depth = lax.axis_size("cols")
    width, terms = current.shape
    chunks = width // BLOCK
    unit = 8 * 2 * chips * depth
    used = len(block_pairs(width)) * BLOCK
    total = -(-used // unit) * unit
    half = total // 2
    piece = half // chips
    portion = piece // depth

    def floats(*shape):
        return pltpu.VMEM(shape, jnp.float32)

    counts = [chunks, chunks * (chips - 1), chunks * (chips - 1), chunks * depth, chunks, 2, 2 * (chips - 1), 2 * (depth - 1)]
    one_round = [
        pltpu.VMEM((chips, width, 2 * terms), jnp.bfloat16),
        floats(chunks, depth, BLOCK, terms),
        floats(chunks, depth, BLOCK, terms),
        floats(chunks, BLOCK, terms),
        floats(total, BLOCK),
        floats(half, BLOCK),
        floats(chips - 1, piece, BLOCK),
        floats(depth - 1, portion, BLOCK),
        floats(total, BLOCK),
    ] + [pltpu.SemaphoreType.DMA((count,)) for count in counts for _ in range(2)]
    return pl.pallas_call(
        functools.partial(iterate_kernel, chips, depth),
        out_shape=jax.ShapeDtypeStruct((width, terms), jnp.float32),
        in_specs=[VMEM] * 3,
        out_specs=VMEM,
        scratch_shapes=[floats(width, terms), floats(width, width + terms), floats(BLOCK, 2 * BLOCK)] + one_round * ITERS,
        compiler_params=pltpu.CompilerParams(
            collective_id=0, has_side_effects=True, vmem_limit_bytes=56 * 2**20
        ),
    )(current, high, low)


def local(basis, tile_counts, tile_rows, tile_cols, tile_live, marginals):
    terms_here = basis.shape[1]
    row_count = lax.axis_size("rows")
    col_count = lax.axis_size("cols")
    row_index = lax.axis_index("rows")
    col_index = lax.axis_index("cols")
    group_size = row_count * terms_here
    marg_float = marginals.astype(jnp.float32)
    log_total = jnp.log(jnp.sum(marg_float)).reshape(1)
    log_margins = jnp.log(marg_float)
    row_logs = lax.dynamic_index_in_dim(
        log_margins.reshape(col_count, row_count, terms_here), row_index, 1, keepdims=False
    ).reshape(-1, 1)
    col_logs = lax.dynamic_slice_in_dim(log_margins, col_index * group_size, group_size).reshape(1, -1)
    high, low = build_matrix(tile_rows, tile_cols, tile_live, log_total, tile_counts, row_logs, col_logs)
    return iterate(basis, high, low)


def solution(mesh):
    in_specs = (
        P(None, ("cols", "rows")),
        P(("rows", "cols"), None, None),
        P(("rows", "cols")),
        P(("rows", "cols")),
        P(("rows", "cols")),
        P(),
    )
    out_specs = P(None, ("cols", "rows"))
    return jax.shard_map(local, mesh=mesh, in_specs=in_specs, out_specs=out_specs, check_vma=False)
```

```python
import functools

import jax
import jax.numpy as jnp
from jax import lax
from jax.experimental import pallas as pl
from jax.experimental.pallas import tpu as pltpu
from jax.sharding import PartitionSpec as P

ITERS = 2
HIGHEST = lax.Precision.HIGHEST
MESH = pl.DeviceIdType.MESH
VMEM = pl.BlockSpec(memory_space=pltpu.VMEM)
SMEM = pl.BlockSpec(memory_space=pltpu.SMEM)
BLOCK = 128
PANEL = 16


def dot_nt(left, right, precision=HIGHEST):
    return lax.dot_general(
        left, right, (((1,), (1,)), ((), ())), precision=precision, preferred_element_type=jnp.float32
    )


def dot_tn(left, right):
    return lax.dot_general(
        left, right, (((0,), (0,)), ((), ())), precision=HIGHEST, preferred_element_type=jnp.float32
    )


def dot_nn(left, right):
    return jnp.dot(left, right, precision=HIGHEST, preferred_element_type=jnp.float32)


def matrix_kernel(rows_ref, cols_ref, live_ref, total_ref, counts_ref, row_logs_ref, col_logs_ref, high_ref, low_ref, dense):
    tile = counts_ref.shape[1]
    log_total = total_ref[0]
    dense[...] = jnp.zeros_like(dense)

    def add_tile(slot, carry):
        row = pl.multiple_of(rows_ref[slot] * tile, tile)
        col = pl.multiple_of(cols_ref[slot] * tile, tile)
        counts = counts_ref[slot]
        ratio = (
            jnp.log(jnp.maximum(counts.astype(jnp.float32), 1.0))
            + log_total
            - row_logs_ref[pl.ds(row, tile), :]
            - col_logs_ref[:, pl.ds(col, tile)]
        )
        value = jnp.where(counts > 0, jnp.maximum(ratio, 0.0), 0.0)
        value = value.astype(jnp.bfloat16).astype(jnp.float32)
        dense[pl.ds(row, tile), pl.ds(col, tile)] += value
        return carry

    lax.fori_loop(0, live_ref[0], add_tile, 0)

    def split(block, carry):
        here = pl.ds(pl.multiple_of(block * tile, tile), tile)
        whole = dense[here, :]
        high = whole.astype(jnp.bfloat16)
        high_ref[here, :] = high
        low_ref[here, :] = (whole - high.astype(jnp.float32)).astype(jnp.bfloat16)
        return carry

    lax.fori_loop(0, dense.shape[0] // tile, split, 0)


def build_matrix(tile_rows, tile_cols, tile_live, log_total, tile_counts, row_logs, col_logs):
    shape = (row_logs.shape[0], col_logs.shape[1])
    return pl.pallas_call(
        matrix_kernel,
        out_shape=[jax.ShapeDtypeStruct(shape, jnp.bfloat16)] * 2,
        in_specs=[SMEM] * 4 + [VMEM] * 3,
        out_specs=[VMEM] * 2,
        scratch_shapes=[pltpu.VMEM(shape, jnp.float32)],
        compiler_params=pltpu.CompilerParams(vmem_limit_bytes=56 * 2**20),
    )(tile_rows, tile_cols, tile_live, log_total, tile_counts, row_logs, col_logs)


def block_pairs(width):
    count = width // BLOCK
    return [(i, j) for i in range(count) for j in range(i, count)]


def iterate_kernel(chips, depth, cur_ref, high_ref, low_ref, out_ref, share, work, small, *rounds):
    row = lax.axis_index("rows")
    level = lax.axis_index("cols")
    chip = row // 2
    core = row % 2
    sibling = {"rows": chip * 2 + (1 - core), "cols": level}
    plane = [{"rows": lax.rem(chip + k, chips) * 2 + core, "cols": level} for k in range(1, chips)]
    column = [{"rows": row, "cols": lax.rem(level + k, depth)} for k in range(1, depth)]
    peers = [sibling] + plane + column
    above, below = column[0], column[depth - 2]
    barrier = pltpu.get_barrier_semaphore()
    for peer in peers:
        pl.semaphore_signal(barrier, inc=1, device_id=peer, device_id_type=MESH)
    width, terms = cur_ref.shape
    chunk = BLOCK
    chunks = width // chunk
    others = chips - 1
    last = depth - 1
    pair = 2 * terms
    pairs = block_pairs(width)
    lanes = pl.ds(pl.multiple_of(core * terms, terms), terms)

    def rows_at(start, size):
        return pl.ds(pl.multiple_of(start, 8), size)

    def block_at(index):
        return pl.ds(pl.multiple_of(index * BLOCK, BLOCK), BLOCK)

    def remote(source, target, sent, received, peer):
        return pltpu.make_async_remote_copy(
            src_ref=source,
            dst_ref=target,
            send_sem=sent,
            recv_sem=received,
            device_id=peer,
            device_id_type=MESH,
        )

    def send(source, target, sends, receives, index, peer):
        copy = remote(source, target, sends.at[index], receives.at[index], peer)
        copy.start()
        return copy

    def each(count, step):
        def body(index, carry):
            step(index)
            return carry

        lax.fori_loop(0, count, body, 0)

    def make_round(
        basis, part, inbox, relay, mine, core_in, plane_in, z_in, gram,
        near_send, near_recv, far_send, far_recv, pass_send, pass_recv, sum_send, sum_recv, relay_send, relay_recv,
        core_send, core_recv, plane_send, plane_recv, z_send, z_recv,
    ):
        def near_copy(q):
            own = basis.at[chip, block_at(q), lanes]
            return remote(own, own, near_send.at[q], near_recv.at[q], sibling)

        def far_copy(q, k):
            own = basis.at[chip, block_at(q), lanes]
            index = q * others + k
            return remote(own, own, far_send.at[index], far_recv.at[index], plane[k])

        def pass_copy(q, k):
            there = basis.at[lax.rem(chip + others - k, chips), block_at(q), lanes]
            index = q * others + k
            return remote(there, there, pass_send.at[index], pass_recv.at[index], sibling)

        def direct_copy(q, k):
            return remote(part.at[q, lax.rem(level + k, depth)], inbox.at[q, level], sum_send.at[q * depth + k], sum_recv.at[q * depth + level], column[k - 1])

        def relay_copy(q, target, peer):
            return remote(part.at[q, target], relay.at[q], relay_send.at[q], relay_recv.at[q], peer)

        def gather(q, vectors):
            basis[chip, block_at(q), lanes] = vectors.astype(jnp.bfloat16)
            for k in range(others):
                far_copy(q, k).start()
            near_copy(q).start()

        def forward(q):
            for k in range(others):
                far_copy(q, k).wait_recv()
                pass_copy(q, k).start()

        def multiply(q):
            near_copy(q).wait_recv()
            total = None
            for k in range(chips):
                if k:
                    pass_copy(q, k - 1).wait_recv()
                source = lax.rem(chip + chips - k, chips)
                columns = pl.ds(pl.multiple_of(source * pair, pair), pair)
                vectors = basis[source, block_at(q), :]
                product = dot_nt(high_ref[:, columns], vectors, None) + dot_nt(low_ref[:, columns], vectors, None)
                total = product if total is None else total + product
            for l in range(depth):
                part[q, l] = total[l * terms : (l + 1) * terms, :]

            @pl.when(level == 0)
            def _():
                relay_copy(q, last, above).start()

            @pl.when(level == last)
            def _():
                relay_copy(q, 0, below).start()

            for k in range(1, depth):
                target = lax.rem(level + k, depth)
                waits = ((level <= 1) & (target == last)) | ((level >= last - 1) & (target == 0))

                @pl.when(jnp.logical_not(waits))
                def _():
                    direct_copy(q, k).start()

        def pass_relay(q):
            @pl.when(level == 1)
            def _():
                relay_copy(q, last, above).wait_recv()
                part[q, last] += relay[q]
                direct_copy(q, last - 1).start()

            @pl.when(level == last - 1)
            def _():
                relay_copy(q, 0, below).wait_recv()
                part[q, 0] += relay[q]
                direct_copy(q, 2).start()

        def collect(q):
            share[block_at(q), :] = part[q, level]
            for u in range(depth):
                absent = (level == u) | ((level == last) & (u == 0)) | ((level == 0) & (u == last))

                @pl.when(jnp.logical_not(absent))
                def _():
                    remote(part.at[q, u], inbox.at[q, u], sum_send.at[q * depth], sum_recv.at[q * depth + u], above).wait_recv()
                    share[block_at(q), :] += inbox[q, u]

            share[block_at(q), :] = share[block_at(q), :].T

        def wait_sent(q):
            near_copy(q).wait_send()
            for k in range(others):
                far_copy(q, k).wait_send()
                pass_copy(q, k).wait_send()
            for k in range(1, depth):
                by_relay = ((level == 0) & (k == last)) | ((level == last) & (k == 1))

                @pl.when(jnp.logical_not(by_relay))
                def _():
                    direct_copy(q, k).wait_send()

            @pl.when(level == 0)
            def _():
                relay_copy(q, last, above).wait_send()

            @pl.when(level == last)
            def _():
                relay_copy(q, 0, below).wait_send()

        def reduce_gram():
            total = mine.shape[0]
            half = total // 2
            piece = half // chips
            portion = piece // depth
            for index, (i, j) in enumerate(pairs):
                mine[index * BLOCK : (index + 1) * BLOCK, :] = dot_nt(
                    share[i * BLOCK : (i + 1) * BLOCK, :], share[j * BLOCK : (j + 1) * BLOCK, :]
                )
            used = len(pairs) * BLOCK
            if used < total:
                mine[used:, :] = jnp.zeros((total - used, BLOCK), jnp.float32)

            half_start = core * half
            first = send(mine.at[rows_at((1 - core) * half, half)], core_in, core_send, core_recv, 0, sibling)
            first.wait()
            mine[rows_at(half_start, half), :] += core_in[...]

            piece_start = half_start + chip * piece
            copies = [
                send(mine.at[rows_at(half_start + lax.rem(chip + k, chips) * piece, piece)], plane_in.at[k - 1], plane_send, plane_recv, k - 1, plane[k - 1])
                for k in range(1, chips)
            ]
            each(chunks // 2, wait_sent)
            for copy in copies:
                copy.wait()
            summed = mine[rows_at(piece_start, piece), :]
            for k in range(1, chips):
                summed += plane_in[k - 1]
            mine[rows_at(piece_start, piece), :] = summed

            part_start = piece_start + level * portion
            copies = [
                send(mine.at[rows_at(piece_start + lax.rem(level + k, depth) * portion, portion)], z_in.at[k - 1], z_send, z_recv, k - 1, column[k - 1])
                for k in range(1, depth)
            ]
            each(chunks - chunks // 2, lambda q: wait_sent(q + chunks // 2))
            for copy in copies:
                copy.wait()
            summed = mine[rows_at(part_start, portion), :]
            for k in range(1, depth):
                summed += z_in[k - 1]
            gram[rows_at(part_start, portion), :] = summed

            here = gram.at[rows_at(part_start, portion)]
            copies = [
                send(here, here, z_send, z_recv, depth - 2 + k, column[k - 1]) for k in range(1, depth)
            ]
            for copy in copies:
                copy.wait()
            here = gram.at[rows_at(piece_start, piece)]
            copies = [
                send(here, here, plane_send, plane_recv, chips - 2 + k, plane[k - 1]) for k in range(1, chips)
            ]
            for copy in copies:
                copy.wait()
            here = gram.at[rows_at(half_start, half)]
            send(here, here, core_send, core_recv, 1, sibling).wait()
            for index, (i, j) in enumerate(pairs):
                work[i * BLOCK : (i + 1) * BLOCK, j * BLOCK : (j + 1) * BLOCK] = gram[index * BLOCK : (index + 1) * BLOCK, :]
            work[:, width:] = share[...]

        return gather, forward, multiply, pass_relay, collect, reduce_gram

    sublane = lax.broadcasted_iota(jnp.int32, (PANEL, BLOCK), 0)
    unit = (
        lax.broadcasted_iota(jnp.int32, (BLOCK, BLOCK), 0) == lax.broadcasted_iota(jnp.int32, (BLOCK, BLOCK), 1)
    ).astype(jnp.float32)

    def eliminate(b):
        here = block_at(b)
        small[:, :BLOCK] = work[here, here]
        small[:, BLOCK:] = unit
        for start in range(0, BLOCK, PANEL):
            left = small[start : start + PANEL, :BLOCK]
            right = small[start : start + PANEL, BLOCK:]
            spread = [
                jnp.broadcast_to(left[:, start + k : start + k + 1], (PANEL, BLOCK)) for k in range(PANEL)
            ]
            for i in range(PANEL):
                inverse = lax.rsqrt(spread[i][i : i + 1, :])
                left_row = left[i : i + 1, :] * inverse
                right_row = right[i : i + 1, :] * inverse
                scale = jnp.where(sublane > i, spread[i] * inverse, 0.0)
                left = jnp.where(sublane == i, left_row, left - scale * left_row)
                right = jnp.where(sublane == i, right_row, right - scale * right_row)
                for k in range(i + 1, PANEL):
                    spread[k] = spread[k] - scale * (spread[k][i : i + 1, :] * inverse)
            small[start : start + PANEL, :BLOCK] = left
            small[start : start + PANEL, BLOCK:] = right
            rest = start + PANEL
            if rest < BLOCK:
                both = small[start : start + PANEL, :]
                small[rest:, :] -= dot_tn(left, both)[rest:, :]
        solved = dot_nn(small[:, BLOCK:], work[here, :])
        work[here, :] = solved
        return solved[:, width:]

    def update(b):
        def body(i, carry):
            work[block_at(i), :] -= dot_tn(work[block_at(b), block_at(i)], work[block_at(b), :])
            return carry

        lax.fori_loop(b + 1, chunks, body, 0)

    per = len(rounds) // ITERS
    parts = [make_round(*rounds[it * per : (it + 1) * per]) for it in range(ITERS)]
    pl.semaphore_wait(barrier, len(peers))
    gather, forward, multiply, pass_relay = parts[0][:4]
    each(chunks, lambda q: gather(q, cur_ref[block_at(q), :]))
    forward(0)

    def first_step(q):
        forward(q + 1)
        multiply(q)

        @pl.when(q > 0)
        def _():
            pass_relay(q - 1)

    each(chunks - 1, first_step)
    multiply(chunks - 1)
    pass_relay(chunks - 2)
    pass_relay(chunks - 1)
    for it in range(ITERS):
        collect, reduce_gram = parts[it][4:]
        each(chunks, collect)
        reduce_gram()
        if it + 1 < ITERS:
            gather, forward, multiply, pass_relay = parts[it + 1][:4]

            def step(b):
                solved = eliminate(b)
                gather(b, solved)

                @pl.when(b > 0)
                def _():
                    forward(b - 1)

                update(b)

                @pl.when(b > 0)
                def _():
                    multiply(b - 1)

                @pl.when(b > 1)
                def _():
                    pass_relay(b - 2)

            each(chunks, step)
            forward(chunks - 1)
            pass_relay(chunks - 2)
            multiply(chunks - 1)
            pass_relay(chunks - 1)
        else:

            def final(b):
                out_ref[block_at(b), :] = eliminate(b)
                update(b)

            each(chunks, final)


def iterate(current, high, low):
    chips = lax.axis_size("rows") // 2
    depth = lax.axis_size("cols")
    width, terms = current.shape
    chunks = width // BLOCK
    unit = 8 * 2 * chips * depth
    used = len(block_pairs(width)) * BLOCK
    total = -(-used // unit) * unit
    half = total // 2
    piece = half // chips
    portion = piece // depth

    def floats(*shape):
        return pltpu.VMEM(shape, jnp.float32)

    counts = [chunks, chunks * (chips - 1), chunks * (chips - 1), chunks * depth, chunks, 2, 2 * (chips - 1), 2 * (depth - 1)]
    one_round = [
        pltpu.VMEM((chips, width, 2 * terms), jnp.bfloat16),
        floats(chunks, depth, BLOCK, terms),
        floats(chunks, depth, BLOCK, terms),
        floats(chunks, BLOCK, terms),
        floats(total, BLOCK),
        floats(half, BLOCK),
        floats(chips - 1, piece, BLOCK),
        floats(depth - 1, portion, BLOCK),
        floats(total, BLOCK),
    ] + [pltpu.SemaphoreType.DMA((count,)) for count in counts for _ in range(2)]
    return pl.pallas_call(
        functools.partial(iterate_kernel, chips, depth),
        out_shape=jax.ShapeDtypeStruct((width, terms), jnp.float32),
        in_specs=[VMEM] * 3,
        out_specs=VMEM,
        scratch_shapes=[floats(width, terms), floats(width, width + terms), floats(BLOCK, 2 * BLOCK)] + one_round * ITERS,
        compiler_params=pltpu.CompilerParams(
            collective_id=0, has_side_effects=True, vmem_limit_bytes=56 * 2**20
        ),
    )(current, high, low)


def local(basis, tile_counts, tile_rows, tile_cols, tile_live, marginals):
    terms_here = basis.shape[1]
    row_count = lax.axis_size("rows")
    col_count = lax.axis_size("cols")
    row_index = lax.axis_index("rows")
    col_index = lax.axis_index("cols")
    group_size = row_count * terms_here
    marg_float = marginals.astype(jnp.float32)
    log_total = jnp.log(jnp.sum(marg_float)).reshape(1)
    log_margins = jnp.log(marg_float)
    row_logs = lax.dynamic_index_in_dim(
        log_margins.reshape(col_count, row_count, terms_here), row_index, 1, keepdims=False
    ).reshape(-1, 1)
    col_logs = lax.dynamic_slice_in_dim(log_margins, col_index * group_size, group_size).reshape(1, -1)
    high, low = build_matrix(tile_rows, tile_cols, tile_live, log_total, tile_counts, row_logs, col_logs)
    return iterate(basis, high, low)


def solution(mesh):
    in_specs = (
        P(None, ("cols", "rows")),
        P(("rows", "cols"), None, None),
        P(("rows", "cols")),
        P(("rows", "cols")),
        P(("rows", "cols")),
        P(),
    )
    out_specs = P(None, ("cols", "rows"))
    return jax.shard_map(local, mesh=mesh, in_specs=in_specs, out_specs=out_specs, check_vma=False)
```
